32 devices in a mesh: grp: 2 (over y), inp: 8 (over z, x), freq: 2 (over core).
Axes of the slice: x: 2, y: 2, z: 4, core: 2. Of those that a mesh axis runs over, the one named last changes fastest.
Arguments:
- voltages: int32 [2048, 64, 2048], P(('grp', 'inp'), 'freq'), parts along dimension 0, may hold values from -127 to 127, as said below
- coeffs: int32 [8, 2048], replicated, may hold values from -6144 to 6144, as said below
Outputs:
- visibilities: bfloat16 [1024, 2, 36, 128, 128], P(('grp', 'inp', 'freq')), parts along dimension 0
The draws below stay inside these ranges and needn't reach their ends.
There are 2 independent parts, one for each index of `grp`. The reference program is written for one: setup_inputs(seed, part) draws one part's arguments, and reference() takes and returns one part's arrays. A program takes and returns all parts, laid end to end along the dimension named above; an argument that names none is the same for every part. Nothing has to cross between parts.
Inputs may be any that keep to these rules, and one draw needn't show every extreme that they name: `voltages`: signed 8-bit samples. `coeffs`: integer coefficients.
All inputs are finite; a program needn't handle non-finite values.
Results may differ from the reference program's by a relative error of at most 0.0069.
Values may be sent and summed in bfloat16 or wider, within the bound.
No kernel may reach another device: no remote copies, remote signals or barrier semaphores. Data moves between devices by JAX's collectives and lax.ppermute only.
A program may use at most 384 MiB of HBM per device.

```python
import math
import jax
import jax.numpy as jnp
from jax import lax

SPF = 2048
TAPS = 8
CH = 512
CH0 = 256
INPUTS = 1024
BLK = 128
NBLK = 8
FRAMES = 64


def draw_voltages(key, part):
    key_base, key_values = jax.random.split(jax.random.fold_in(key, 11))
    base = jax.random.randint(key_base, (INPUTS, 1, 1), 4, 32)
    frame = jnp.arange(FRAMES, dtype=jnp.int32)[None, :, None]
    limit = base * (FRAMES + 3 * frame) // FRAMES
    limit = jnp.broadcast_to(limit, (INPUTS, FRAMES, SPF))
    return jax.random.randint(key_values, (INPUTS, FRAMES, SPF), -limit, limit + 1).astype(jnp.int32)


def draw_coeffs(key, part):
    length = TAPS * SPF
    place = jnp.arange(length, dtype=jnp.int32)
    tent = jnp.minimum(place + 1, length - place) * 8192 // length
    tap = place // SPF
    sign = 1 - 2 * (jnp.abs(2 * tap - (TAPS - 1)) // 2 % 2)
    noise = jax.random.randint(jax.random.fold_in(key, 23), (length,), -(tent // 2), tent // 2 + 1)
    return (sign * tent + noise).reshape(TAPS, SPF).astype(jnp.int32)


def setup_inputs(seed: int = 0, part: int = 0) -> dict:
    streams_of = jax.random.split(jax.random.key(seed), 3)
    own_keys = jax.random.split(jax.random.fold_in(streams_of[2], part), 3)
    voltages = draw_voltages(jax.random.fold_in(jax.random.fold_in(streams_of[2], part), 71), part)
    coeffs = draw_coeffs(jax.random.fold_in(streams_of[2], 71), part)
    return dict(voltages=voltages, coeffs=coeffs)


def make_table():
    sample = jnp.arange(SPF, dtype=jnp.int32)[:, None]
    channel = jnp.arange(CH, dtype=jnp.int32)[None, :] + CH0
    phase = sample * channel % SPF
    angle = phase.astype(jnp.float32) * (2.0 * math.pi / SPF)
    return jnp.concatenate([jnp.cos(angle), -jnp.sin(angle)], axis=1).astype(jnp.bfloat16)

def block_pairs():
    return [(row_index, col_index) for row_index in range(NBLK) for col_index in range(row_index, NBLK)]

def reference(voltages, coeffs):
    dft_table = make_table().astype(jnp.float32)
    weights = coeffs.astype(jnp.float32)

    def front_end(samples):
        padded = jnp.pad(samples.astype(jnp.float32), ((0, 0), (TAPS - 1, 0), (0, 0)))
        summed = jnp.zeros((samples.shape[0], FRAMES, SPF), jnp.float32)
        for tap_index in range(TAPS):
            begin = TAPS - 1 - tap_index
            summed = summed + weights[tap_index] * padded[:, begin:begin + FRAMES, :]
        rounded = lax.optimization_barrier(summed.astype(jnp.bfloat16))
        filtered = rounded.astype(jnp.float32)
        spectrum = jnp.dot(filtered.reshape(-1, SPF), dft_table, precision=lax.Precision.HIGHEST, preferred_element_type=jnp.float32).reshape(-1, FRAMES, 2 * CH)
        power = lax.optimization_barrier(jnp.sum(spectrum * spectrum, axis=(1, 2))) / (FRAMES * CH)
        gains = 1.0 / jnp.sqrt(power + 1e-06)
        return (spectrum * gains[:, None, None]).astype(jnp.bfloat16)
    blocked = voltages.reshape(NBLK, BLK, FRAMES, SPF)
    scaled = lax.map(front_end, blocked).reshape(INPUTS, FRAMES, 2, CH)
    stacked = jnp.transpose(scaled, (3, 0, 2, 1)).reshape(CH, INPUTS, 2 * FRAMES)
    pairs = block_pairs()

    def correlate(operand):
        first = operand.astype(jnp.float32)
        second = jnp.concatenate([-first[:, FRAMES:], first[:, :FRAMES]], axis=1)
        real_part = jnp.dot(first, first.T, precision=lax.Precision.HIGHEST, preferred_element_type=jnp.float32)
        imag_part = jnp.dot(first, second.T, precision=lax.Precision.HIGHEST, preferred_element_type=jnp.float32)
        grams = jnp.stack([real_part, imag_part]) * (1.0 / FRAMES)
        picked = jnp.stack([grams[:, row_index * BLK:(row_index + 1) * BLK, col_index * BLK:(col_index + 1) * BLK] for row_index, col_index in pairs], axis=1)
        return picked.astype(jnp.bfloat16)
    return lax.map(correlate, stacked)
```

```python
import math

import jax
import jax.numpy as jnp
import ml_dtypes
import numpy as np
from jax import lax
from jax.experimental import pallas as pl
from jax.experimental.pallas import tpu as pltpu
from jax.sharding import PartitionSpec as P

SPF = 2048
TAPS = 8
CH = 512
CH0 = 256
INPUTS = 1024
BLK = 128
LANES = 128
UBLK = 16
TBLK = 16
HALVES = 2


def passed_along(x, axis, by):
    length = lax.axis_size(axis)
    pairs = [(i, i + by) for i in range(length) if 0 <= i + by < length]
    return lax.ppermute(x, axis, pairs)


def make_table():
    sample = jnp.arange(SPF, dtype=jnp.int32)[:, None]
    channel = jnp.arange(CH, dtype=jnp.int32)[None, :] + CH0
    phase = sample * channel % SPF
    angle = phase.astype(jnp.float32) * (2.0 * math.pi / SPF)
    return jnp.concatenate([jnp.cos(angle), -jnp.sin(angle)], axis=1).astype(jnp.bfloat16)


def any_sizes(voltages, coeffs):
    inputs_here = voltages.shape[0]
    frames_here = voltages.shape[1]
    inp_count = lax.axis_size("inp")
    freq_count = lax.axis_size("freq")
    frames_all = frames_here * freq_count
    history = voltages[:, frames_here - (TAPS - 1) :, :].astype(jnp.bfloat16)
    earlier = passed_along(history, "freq", 1)
    extended = jnp.concatenate([earlier.astype(jnp.float32), voltages.astype(jnp.float32)], axis=1)
    weights = coeffs.astype(jnp.float32)
    summed = jnp.zeros((inputs_here, frames_here, SPF), jnp.float32)
    for tap_index in range(TAPS):
        begin = TAPS - 1 - tap_index
        summed = summed + weights[tap_index] * extended[:, begin : begin + frames_here, :]
    filtered = summed.astype(jnp.bfloat16).reshape(inputs_here * frames_here, SPF)
    spectrum_t = jnp.einsum("nj,rn->jr", make_table(), filtered, preferred_element_type=jnp.float32)
    spectrum_t = spectrum_t.reshape(2 * CH, inputs_here, frames_here)
    squares = jnp.sum(spectrum_t * spectrum_t, axis=(0, 2))
    power = lax.psum(squares, "freq") / (frames_all * CH)
    gains = 1.0 / jnp.sqrt(power + 1e-06)
    scaled = (spectrum_t * gains[None, :, None]).astype(jnp.bfloat16)
    scaled = scaled.reshape(2, CH, inputs_here * frames_here)
    arrived = lax.all_to_all(scaled[None], ("inp", "freq"), split_axis=2, concat_axis=0, tiled=True)
    width_here = arrived.shape[-2]
    arranged = arrived.reshape(inp_count, freq_count, 2, width_here, inputs_here, frames_here)
    arranged = jnp.transpose(arranged, (3, 0, 4, 2, 1, 5))
    stacked = arranged.reshape(width_here, INPUTS, 2 * frames_all)
    other = jnp.concatenate([-stacked[:, :, frames_all:], stacked[:, :, :frames_all]], axis=2)
    block_count = INPUTS // BLK
    scale = 1.0 / frames_all
    pieces = []
    for row_index in range(block_count):
        row_panel = stacked[:, row_index * BLK : (row_index + 1) * BLK]
        real_part = jnp.einsum(
            "cut,cmt->cum",
            row_panel,
            stacked[:, row_index * BLK :],
            preferred_element_type=jnp.float32,
        )
        imag_part = jnp.einsum(
            "cut,cmt->cum",
            row_panel,
            other[:, row_index * BLK :],
            preferred_element_type=jnp.float32,
        )
        band = jnp.stack([real_part, imag_part], axis=1) * scale
        for col_index in range(row_index, block_count):
            begin = (col_index - row_index) * BLK
            pieces.append(band[:, :, :, begin : begin + BLK])
    return jnp.stack(pieces, axis=2).astype(jnp.bfloat16)


def history_kernel(v_ref, out_ref):
    inputs, frames, _ = v_ref.shape
    flat = v_ref.reshape(inputs * frames, LANES)
    for t in range(frames):
        out_ref[t] = flat[pl.ds(t, inputs, stride=frames), :].astype(jnp.bfloat16)


def last_frames(voltages):
    inputs, frames, _ = voltages.shape
    last = frames // TAPS - 1
    return pl.pallas_call(
        history_kernel,
        name="history",
        grid=(SPF // LANES,),
        in_specs=[pl.BlockSpec((inputs, TAPS, LANES), lambda i: (0, last, i))],
        out_specs=pl.BlockSpec((TAPS, inputs, LANES), lambda i: (0, 0, i)),
        out_shape=jax.ShapeDtypeStruct((TAPS, inputs, SPF), jnp.bfloat16),
    )(voltages)


def filter_kernel(first, near_ref, far_ref, near_c_ref, far_c_ref, *refs):
    even_ref, odd_ref = refs[-2:]
    inputs, frames, _ = near_ref.shape
    sources = []
    for side, (v_ref, c_ref) in enumerate(((near_ref, near_c_ref), (far_ref, far_c_ref))):
        weights = c_ref[...].astype(jnp.float32)
        taps = [jnp.broadcast_to(weights[k : k + 1], (UBLK, LANES)) for k in range(TAPS)]
        hist_ref = refs[side] if first == 0 else None
        sources.append((v_ref.reshape(inputs * frames, LANES), taps, hist_ref))

    def some_inputs(step, carry):
        begin = pl.multiple_of(step * UBLK, UBLK)
        here = pl.ds(begin, UBLK)
        sides = []
        for flat, taps, hist_ref in sources:
            window = []
            made = []
            for t in range(first - TAPS + 1, first + TBLK):
                if t < 0:
                    value = hist_ref[TAPS + t, here, :]
                else:
                    value = flat[pl.ds(begin * frames + t, UBLK, stride=frames), :]
                window.append(value.astype(jnp.float32))
                if t >= first:
                    total = taps[0] * window[-1]
                    for k in range(1, TAPS):
                        total = total + taps[k] * window[-1 - k]
                    made.append(total)
            sides.append(made)
        for t in range(TBLK):
            even_ref[t, here, :] = (sides[0][t] + sides[1][t]).astype(jnp.bfloat16)
            odd_ref[t, here, :] = (sides[0][t] - sides[1][t]).astype(jnp.bfloat16)
        return carry

    lax.fori_loop(0, inputs // UBLK, some_inputs, 0)


def filtered_frames(block, voltages, coeffs, history=None, made=()):
    inputs, frames, _ = voltages.shape
    half = SPF // 2
    steps = half // LANES
    shape = jax.ShapeDtypeStruct((frames, inputs, half), jnp.bfloat16)
    out_spec = pl.BlockSpec((TBLK, inputs, LANES), lambda i: (block, 0, i))
    read = TBLK if block == 0 else frames
    in_specs = [
        pl.BlockSpec((inputs, read, LANES), lambda i: (0, 0, i)),
        pl.BlockSpec((inputs, read, LANES), lambda i: (0, 0, i + steps)),
        pl.BlockSpec((TAPS, LANES), lambda i: (0, i)),
        pl.BlockSpec((TAPS, LANES), lambda i: (0, i + steps)),
    ]
    operands = [voltages, voltages, coeffs, coeffs]
    if block == 0:
        in_specs.append(pl.BlockSpec((TAPS, inputs, LANES), lambda i: (0, 0, i)))
        in_specs.append(pl.BlockSpec((TAPS, inputs, LANES), lambda i: (0, 0, i + steps)))
        operands += [history, history]
    aliases = {}
    for index, array in enumerate(made):
        aliases[len(operands)] = index
        in_specs.append(pl.BlockSpec(memory_space=pl.ANY))
        operands.append(array)

    def kernel(*refs):
        filter_kernel(block * TBLK, *refs)

    return pl.pallas_call(
        kernel,
        name=f"filter_{block}",
        grid=(steps,),
        in_specs=in_specs,
        out_specs=[out_spec, out_spec],
        out_shape=[shape, shape],
        input_output_aliases=aliases,
        compiler_params=pltpu.CompilerParams(vmem_limit_bytes=40 * 2**20),
    )(*operands)


def chunk_tables(parts, width):
    depth = width // (2 * HALVES)
    tables = []
    for parity in range(2):
        for piece in range(HALVES):
            within = 2 * (piece * depth + np.arange(depth)) + parity
            channel = (np.arange(parts)[:, None] * width + within[None, :]).reshape(-1) + CH0
            phase = channel[:, None].astype(np.int64) * np.arange(SPF // 2)[None, :] % SPF
            angle = phase.astype(np.float32) * np.float32(2.0 * math.pi / SPF)
            wide = angle.astype(np.float64)
            both = np.stack([np.cos(wide), -np.sin(wide)], axis=1)
            both = both.reshape(-1, SPF // 2).astype(np.float32)
            tables.append(jnp.asarray(both.astype(ml_dtypes.bfloat16)))
    return tables


def transform_kernel(parts, me_ref, x_ref, table_ref, *refs):
    outs, power_ref, turned = refs[:parts], refs[parts], refs[parts + 1]
    rows = table_ref.shape[0]
    own = rows // parts
    spectrum = lax.dot_general(
        table_ref[...],
        x_ref[...].reshape(TBLK * BLK, SPF // 2),
        (((1,), (1,)), ((), ())),
        preferred_element_type=jnp.float32,
    )
    square = jnp.zeros((8, BLK), jnp.float32)
    for t in range(TBLK):
        frame = spectrum[:, t * BLK : (t + 1) * BLK]
        turned[pl.ds(t, rows, stride=TBLK), :] = frame
        square = square + jnp.sum((frame * frame).reshape(rows // 8, 8, BLK), axis=0)

    @pl.when(pl.program_id(0) == 0)
    def _():
        power_ref[...] = square

    @pl.when(pl.program_id(0) != 0)
    def _():
        power_ref[...] += square

    me = me_ref[0]
    for s in range(parts):
        there = jnp.bitwise_xor(me, s)
        begin = pl.multiple_of(there * (own * TBLK), own * TBLK)
        mine = turned[pl.ds(begin, own * TBLK), :]
        outs[s][...] = mine.reshape(outs[s].shape).astype(jnp.bfloat16)


def transformed(name, parts, me, x, table):
    frames, inputs, _ = x.shape
    rows = table.shape[0]
    depth = rows // parts // 2
    steps = frames // TBLK
    message = jax.ShapeDtypeStruct((steps, depth, 2 * TBLK, BLK), jnp.bfloat16)

    def kernel(me_ref, x_ref, table_ref, *refs):
        transform_kernel(parts, me_ref, x_ref, table_ref, *refs)

    out = pl.pallas_call(
        kernel,
        name=name,
        grid_spec=pltpu.PrefetchScalarGridSpec(
            num_scalar_prefetch=1,
            grid=(steps,),
            in_specs=[
                pl.BlockSpec((TBLK, inputs, SPF // 2), lambda i, me: (i, 0, 0)),
                pl.BlockSpec((rows, SPF // 2), lambda i, me: (0, 0)),
            ],
            out_specs=[
                pl.BlockSpec((1, depth, 2 * TBLK, BLK), lambda i, me: (i, 0, 0, 0))
                for _ in range(parts)
            ]
            + [pl.BlockSpec((8, BLK), lambda i, me: (0, 0))],
            scratch_shapes=[pltpu.VMEM((rows * TBLK, BLK), jnp.float32)],
        ),
        out_shape=[message] * parts + [jax.ShapeDtypeStruct((8, BLK), jnp.float32)],
        compiler_params=pltpu.CompilerParams(vmem_limit_bytes=40 * 2**20),
    )(me, x, table)
    return out[:parts], out[parts]


def correlate_kernel(parts, steps, me_ref, *refs):
    messages = refs[:parts]
    row_ref = refs[parts]
    out_ref, plain, other, columns = refs[-4:]
    blocks = INPUTS // BLK
    freq = parts // blocks
    span = steps * 2 * TBLK
    me = me_ref[0]

    @pl.when(pl.program_id(0) == 0)
    def _():
        for r in range(blocks):
            wide = jnp.broadcast_to(row_ref[r : r + 1, :], (BLK, BLK))
            columns[r * BLK : (r + 1) * BLK, :] = wide.T

    for s in range(parts):
        source = jnp.bitwise_xor(me, s)
        block, place = source // freq, source % freq
        for step in range(steps):
            begin = pl.multiple_of(place * span + step * 2 * TBLK, 2 * TBLK)
            real = messages[s][step, 0, :TBLK, :]
            imag = messages[s][step, 0, TBLK:, :]
            plain[block, pl.ds(begin, TBLK), :] = real
            plain[block, pl.ds(begin + TBLK, TBLK), :] = imag
            other[block, pl.ds(begin, TBLK), :] = -imag
            other[block, pl.ds(begin + TBLK, TBLK), :] = real

    sides = [plain[r].T for r in range(blocks)]
    for c in range(blocks):
        weights = jnp.concatenate([plain[c], other[c]], axis=1)
        lhs = sides[0] if c == 0 else jnp.concatenate(sides[: c + 1], axis=0)
        both = jnp.dot(lhs, weights, preferred_element_type=jnp.float32)
        row_gain = row_ref[c : c + 1, :]
        for r in range(c + 1):
            pair = r * blocks - r * (r - 1) // 2 + (c - r)
            gain = columns[r * BLK : (r + 1) * BLK, :] * (row_gain * (1.0 / (freq * steps * TBLK)))
            for part in range(2):
                piece = both[r * BLK : (r + 1) * BLK, part * BLK : (part + 1) * BLK]
                out_ref[0, part, pair] = (piece * gain).astype(jnp.bfloat16)


def correlated(name, me, messages, gains, chunk, width, before=None):
    parts = len(messages)
    steps, depth, _, _ = messages[0].shape
    blocks = INPUTS // BLK
    pairs = blocks * (blocks + 1) // 2
    parity, piece = chunk // HALVES, chunk % HALVES
    span = parts // blocks * steps * 2 * TBLK
    in_specs = [
        pl.BlockSpec((steps, 1, 2 * TBLK, BLK), lambda i, me: (0, i, 0, 0)) for _ in range(parts)
    ] + [pl.BlockSpec((blocks, BLK), lambda i, me: (0, 0))]
    operands = [me, *messages, gains]
    aliases = {}
    if before is not None:
        aliases[len(operands)] = 0
        in_specs.append(pl.BlockSpec(memory_space=pl.ANY))
        operands.append(before)

    def kernel(me_ref, *refs):
        correlate_kernel(parts, steps, me_ref, *refs)

    return pl.pallas_call(
        kernel,
        name=name,
        grid_spec=pltpu.PrefetchScalarGridSpec(
            num_scalar_prefetch=1,
            grid=(depth,),
            in_specs=in_specs,
            out_specs=pl.BlockSpec(
                (1, 2, pairs, BLK, BLK),
                lambda i, me: (2 * (piece * depth + i) + parity, 0, 0, 0, 0),
            ),
            scratch_shapes=[
                pltpu.VMEM((blocks, span, BLK), jnp.bfloat16),
                pltpu.VMEM((blocks, span, BLK), jnp.bfloat16),
                pltpu.VMEM((INPUTS, BLK), jnp.float32),
            ],
        ),
        out_shape=jax.ShapeDtypeStruct((width, 2, pairs, BLK, BLK), jnp.bfloat16),
        input_output_aliases=aliases,
        compiler_params=pltpu.CompilerParams(vmem_limit_bytes=40 * 2**20),
    )(*operands)


def exchanged(messages):
    axes = ("inp", "freq")
    parts = len(messages)
    arrived = [messages[0]]
    for s in range(1, parts):
        pairs = [(i, i ^ s) for i in range(parts)]
        arrived.append(lax.ppermute(messages[s], axes, pairs))
    return arrived


def per_device(voltages, coeffs):
    freq_count = lax.axis_size("freq")
    parts = lax.axis_size("inp") * freq_count
    inputs, frames, _ = voltages.shape
    width = CH // parts
    chunks = 2 * HALVES
    fits = (
        inputs == BLK
        and frames == 2 * TBLK
        and TAPS <= TBLK
        and parts & (parts - 1) == 0
        and width % (2 * HALVES) == 0
        and parts * BLK == INPUTS * freq_count
        and freq_count * frames * 2 == LANES
    )
    if not fits:
        return any_sizes(voltages, coeffs)
    me = lax.axis_index("inp") * freq_count + lax.axis_index("freq")
    me = me.astype(jnp.int32).reshape(1)
    history = passed_along(last_frames(voltages), "freq", 1)
    made = filtered_frames(1, voltages, coeffs)
    made = filtered_frames(0, voltages, coeffs, history, made)
    tables = chunk_tables(parts, width)
    arrived = []
    power = 0.0
    for chunk in range(chunks):
        messages, squares = transformed(
            f"spectra_{chunk}", parts, me, made[chunk // HALVES], tables[chunk]
        )
        power = power + jnp.sum(squares, axis=0)
        arrived.append(exchanged(messages))
    shared = lax.all_gather(power, ("inp", "freq"))
    shared = jnp.sum(shared.reshape(parts // freq_count, freq_count, BLK), axis=1)
    gains = 1.0 / jnp.sqrt(shared / (frames * freq_count * CH) + 1e-06)
    out = None
    for chunk in range(chunks):
        out = correlated(f"correlate_{chunk}", me, arrived[chunk], gains, chunk, width, out)
    return out


def solution(mesh):
    in_specs = (P(("grp", "inp"), "freq", None), P())
    out_specs = P(("grp", "inp", "freq"), None, None, None, None)
    return jax.shard_map(
        per_device, mesh=mesh, in_specs=in_specs, out_specs=out_specs, check_vma=False
    )
```

```python
import math

import jax
import jax.numpy as jnp
import ml_dtypes
import numpy as np
from jax import lax
from jax.experimental import pallas as pl
from jax.experimental.pallas import tpu as pltpu
from jax.sharding import PartitionSpec as P

SPF = 2048
TAPS = 8
CH = 512
CH0 = 256
INPUTS = 1024
BLK = 128
LANES = 128
UBLK = 16
TBLK = 16
PITCH = TBLK + 1


def passed_along(x, axis, by):
    length = lax.axis_size(axis)
    pairs = [(i, i + by) for i in range(length) if 0 <= i + by < length]
    return lax.ppermute(x, axis, pairs)


def make_table():
    sample = jnp.arange(SPF, dtype=jnp.int32)[:, None]
    channel = jnp.arange(CH, dtype=jnp.int32)[None, :] + CH0
    phase = sample * channel % SPF
    angle = phase.astype(jnp.float32) * (2.0 * math.pi / SPF)
    return jnp.concatenate([jnp.cos(angle), -jnp.sin(angle)], axis=1).astype(jnp.bfloat16)


def any_sizes(voltages, coeffs):
    inputs_here = voltages.shape[0]
    frames_here = voltages.shape[1]
    inp_count = lax.axis_size("inp")
    freq_count = lax.axis_size("freq")
    frames_all = frames_here * freq_count
    history = voltages[:, frames_here - (TAPS - 1) :, :].astype(jnp.bfloat16)
    earlier = passed_along(history, "freq", 1)
    extended = jnp.concatenate([earlier.astype(jnp.float32), voltages.astype(jnp.float32)], axis=1)
    weights = coeffs.astype(jnp.float32)
    summed = jnp.zeros((inputs_here, frames_here, SPF), jnp.float32)
    for tap_index in range(TAPS):
        begin = TAPS - 1 - tap_index
        summed = summed + weights[tap_index] * extended[:, begin : begin + frames_here, :]
    filtered = summed.astype(jnp.bfloat16).reshape(inputs_here * frames_here, SPF)
    spectrum_t = jnp.einsum("nj,rn->jr", make_table(), filtered, preferred_element_type=jnp.float32)
    spectrum_t = spectrum_t.reshape(2 * CH, inputs_here, frames_here)
    squares = jnp.sum(spectrum_t * spectrum_t, axis=(0, 2))
    power = lax.psum(squares, "freq") / (frames_all * CH)
    gains = 1.0 / jnp.sqrt(power + 1e-06)
    scaled = (spectrum_t * gains[None, :, None]).astype(jnp.bfloat16)
    scaled = scaled.reshape(2, CH, inputs_here * frames_here)
    arrived = lax.all_to_all(scaled[None], ("inp", "freq"), split_axis=2, concat_axis=0, tiled=True)
    width_here = arrived.shape[-2]
    arranged = arrived.reshape(inp_count, freq_count, 2, width_here, inputs_here, frames_here)
    arranged = jnp.transpose(arranged, (3, 0, 4, 2, 1, 5))
    stacked = arranged.reshape(width_here, INPUTS, 2 * frames_all)
    other = jnp.concatenate([-stacked[:, :, frames_all:], stacked[:, :, :frames_all]], axis=2)
    block_count = INPUTS // BLK
    scale = 1.0 / frames_all
    pieces = []
    for row_index in range(block_count):
        row_panel = stacked[:, row_index * BLK : (row_index + 1) * BLK]
        real_part = jnp.einsum(
            "cut,cmt->cum",
            row_panel,
            stacked[:, row_index * BLK :],
            preferred_element_type=jnp.float32,
        )
        imag_part = jnp.einsum(
            "cut,cmt->cum",
            row_panel,
            other[:, row_index * BLK :],
            preferred_element_type=jnp.float32,
        )
        band = jnp.stack([real_part, imag_part], axis=1) * scale
        for col_index in range(row_index, block_count):
            begin = (col_index - row_index) * BLK
            pieces.append(band[:, :, :, begin : begin + BLK])
    return jnp.stack(pieces, axis=2).astype(jnp.bfloat16)


def turned_over(rows):
    rows = list(rows)
    place = lax.broadcasted_iota(jnp.int32, (8, LANES), 0)
    for shift in (4, 2, 1):
        low = jnp.bitwise_and(place, shift) == 0
        for i in range(8):
            if i & shift == 0:
                near, far = rows[i], rows[i + shift]
                rows[i] = jnp.where(low, near, pltpu.roll(far, shift, 0))
                rows[i + shift] = jnp.where(low, pltpu.roll(near, 8 - shift, 0), far)
    return rows


def frames_of(v_ref, begin):
    groups = []
    for group in range(UBLK // 8):
        groups.append(turned_over([v_ref[begin + group * 8 + i] for i in range(8)]))
    return [[group[t].astype(jnp.float32) for group in groups] for t in range(8)]


def history_kernel(v_ref, out_ref):
    def some_inputs(step, carry):
        begin = pl.multiple_of(step * UBLK, UBLK)
        for t, frame in enumerate(frames_of(v_ref, begin)):
            out_ref[t, pl.ds(begin, UBLK), :] = jnp.concatenate(frame, axis=0).astype(jnp.bfloat16)
        return carry

    lax.fori_loop(0, v_ref.shape[0] // UBLK, some_inputs, 0)


def last_frames(voltages):
    inputs, frames, _ = voltages.shape
    last = frames // TAPS - 1
    return pl.pallas_call(
        history_kernel,
        name="history",
        grid=(SPF // LANES,),
        in_specs=[pl.BlockSpec((inputs, TAPS, LANES), lambda i: (0, last, i))],
        out_specs=pl.BlockSpec((TAPS, inputs, LANES), lambda i: (0, 0, i)),
        out_shape=jax.ShapeDtypeStruct((TAPS, inputs, SPF), jnp.bfloat16),
    )(voltages)


def filter_kernel(block, *refs):
    even_ref, odd_ref = refs[-2:]
    blocks = TBLK // TAPS
    count = blocks + 1
    inputs = even_ref.shape[1]
    groups = UBLK // 8

    def some_inputs(step, carry):
        begin = pl.multiple_of(step * UBLK, UBLK)
        here = pl.ds(begin, UBLK)
        sides = []
        for side in range(2):
            sources = refs[side * count : (side + 1) * count]
            weights = refs[2 * count + side][...].astype(jnp.float32)
            taps = [jnp.broadcast_to(weights[k : k + 1], (8, LANES)) for k in range(TAPS)]
            sides.append((sources, taps))
        before = []
        for sources, _ in sides:
            if block == 0:
                wide = [sources[0][t, here, :].astype(jnp.float32) for t in range(TAPS)]
                before.append([[w[g * 8 : (g + 1) * 8] for g in range(groups)] for w in wide])
            else:
                before.append(frames_of(sources[0], begin))
        for part in range(blocks):
            made = []
            for side, (sources, taps) in enumerate(sides):
                now = frames_of(sources[1 + part], begin)
                window = before[side] + now
                before[side] = now
                totals = []
                for t in range(TAPS):
                    frame = []
                    for g in range(groups):
                        total = taps[0] * window[TAPS + t][g]
                        for k in range(1, TAPS):
                            total = total + taps[k] * window[TAPS + t - k][g]
                        frame.append(total)
                    totals.append(jnp.concatenate(frame, axis=0))
                made.append(totals)
            for t in range(TAPS):
                at = part * TAPS + t
                even_ref[at, here, :] = (made[0][t] + made[1][t]).astype(jnp.bfloat16)
                odd_ref[at, here, :] = (made[0][t] - made[1][t]).astype(jnp.bfloat16)
        return carry

    lax.fori_loop(0, inputs // UBLK, some_inputs, 0)


def filtered_frames(block, voltages, coeffs, history=None):
    inputs, frames, _ = voltages.shape
    half = SPF // 2
    steps = half // LANES
    first = block * (TBLK // TAPS)
    in_specs, operands = [], []
    for side in range(2):
        for place in range(first - 1, first + TBLK // TAPS):
            if place < 0:
                in_specs.append(
                    pl.BlockSpec((TAPS, inputs, LANES), lambda i, side=side: (0, 0, i + side * steps))
                )
                operands.append(history)
            else:
                in_specs.append(
                    pl.BlockSpec(
                        (inputs, TAPS, LANES),
                        lambda i, side=side, place=place: (0, place, i + side * steps),
                    )
                )
                operands.append(voltages)
    for side in range(2):
        in_specs.append(pl.BlockSpec((TAPS, LANES), lambda i, side=side: (0, i + side * steps)))
        operands.append(coeffs)
    shape = jax.ShapeDtypeStruct((TBLK, inputs, half), jnp.bfloat16)
    out_spec = pl.BlockSpec((TBLK, inputs, LANES), lambda i: (0, 0, i))

    def kernel(*refs):
        filter_kernel(block, *refs)

    return pl.pallas_call(
        kernel,
        name=f"filter_{block}",
        grid=(steps,),
        in_specs=in_specs,
        out_specs=[out_spec, out_spec],
        out_shape=[shape, shape],
        compiler_params=pltpu.CompilerParams(vmem_limit_bytes=24 * 2**20),
    )(*operands)


def parity_tables(parts, width):
    tables = []
    for parity in range(2):
        within = np.arange(parity, width, 2)
        channel = (np.arange(parts)[:, None] * width + within[None, :]).reshape(-1) + CH0
        phase = channel[:, None].astype(np.int64) * np.arange(SPF // 2)[None, :] % SPF
        angle = phase.astype(np.float32) * np.float32(2.0 * math.pi / SPF)
        wide = angle.astype(np.float64)
        both = np.stack([np.cos(wide), -np.sin(wide)], axis=1)
        both = both.reshape(-1, SPF // 2).astype(np.float32)
        tables.append(jnp.asarray(both.astype(ml_dtypes.bfloat16)))
    return tables


def transform_kernel(parts, splits, me_ref, late_ref, early_ref, table_ref, *refs):
    outs, power_ref, turned = refs[:-2], refs[-2], refs[-1]
    rows = table_ref.shape[0]
    own = rows // parts
    step = pl.program_id(0)
    me = me_ref[0]

    def work(x_ref):
        spectrum = lax.dot_general(
            table_ref[...],
            x_ref[...].reshape(-1, SPF // 2),
            (((1,), (1,)), ((), ())),
            preferred_element_type=jnp.float32,
        )
        square = jnp.zeros((8, BLK), jnp.float32)
        for t in range(TBLK):
            frame = spectrum[:, t * BLK : (t + 1) * BLK]
            turned[pl.ds(t, rows, stride=PITCH), :] = frame
            square = square + jnp.sum((frame * frame).reshape(rows // 8, 8, BLK), axis=0)
        for s in range(parts):
            there = jnp.bitwise_xor(me, s)
            begin = there * (own * PITCH)
            for split, (first, depth) in enumerate(splits):
                out = outs[split * parts + s]
                for channel in range(depth):
                    for half in range(2):
                        row = (first + channel) * 2 + half
                        value = turned[pl.ds(begin + row * PITCH, TBLK), :]
                        out[0, channel, half * TBLK : (half + 1) * TBLK, :] = value.astype(
                            jnp.bfloat16
                        )
        return square

    @pl.when(step == 0)
    def _():
        power_ref[...] = work(late_ref)

    @pl.when(step == 1)
    def _():
        power_ref[...] += work(early_ref)


def transformed(name, parts, me, late, early, table, splits):
    frames, inputs, _ = late.shape
    rows = table.shape[0]
    shapes, specs = [], []
    for _, depth in splits:
        shapes += [jax.ShapeDtypeStruct((2, depth, 2 * TBLK, BLK), jnp.bfloat16)] * parts
        specs += [
            pl.BlockSpec((1, depth, 2 * TBLK, BLK), lambda i, me: (i, 0, 0, 0))
            for _ in range(parts)
        ]

    def kernel(me_ref, *refs):
        transform_kernel(parts, splits, me_ref, *refs)

    out = pl.pallas_call(
        kernel,
        name=name,
        grid_spec=pltpu.PrefetchScalarGridSpec(
            num_scalar_prefetch=1,
            grid=(2,),
            in_specs=[
                pl.BlockSpec((TBLK, inputs, SPF // 2), lambda i, me: (0, 0, 0)),
                pl.BlockSpec((TBLK, inputs, SPF // 2), lambda i, me: (0, 0, 0)),
                pl.BlockSpec((rows, SPF // 2), lambda i, me: (0, 0)),
            ],
            out_specs=specs + [pl.BlockSpec((8, BLK), lambda i, me: (0, 0))],
            scratch_shapes=[pltpu.VMEM((rows * PITCH + 8, BLK), jnp.float32)],
        ),
        out_shape=shapes + [jax.ShapeDtypeStruct((8, BLK), jnp.float32)],
        compiler_params=pltpu.CompilerParams(vmem_limit_bytes=44 * 2**20),
    )(me, late, early, table)
    messages = [out[split * parts : (split + 1) * parts] for split in range(len(splits))]
    return messages, out[-1]


def correlate_kernel(parts, steps, me_ref, *refs):
    messages = refs[:parts]
    row_ref = refs[parts]
    out_ref, token_ref, plain, other, columns = refs[-5:]
    blocks = INPUTS // BLK
    freq = parts // blocks
    span = steps * 2 * TBLK
    me = me_ref[0]

    @pl.when(pl.program_id(0) == 0)
    def _():
        token_ref[...] = jnp.zeros_like(token_ref)
        for r in range(blocks):
            wide = jnp.broadcast_to(row_ref[r : r + 1, :], (BLK, BLK))
            columns[r * BLK : (r + 1) * BLK, :] = wide.T

    for s in range(parts):
        source = jnp.bitwise_xor(me, s)
        block, place = source // freq, source % freq
        for step in range(steps):
            begin = pl.multiple_of(place * span + step * 2 * TBLK, 2 * TBLK)
            real = messages[s][step, 0, :TBLK, :]
            imag = messages[s][step, 0, TBLK:, :]
            plain[block, pl.ds(begin, TBLK), :] = real
            plain[block, pl.ds(begin + TBLK, TBLK), :] = imag
            other[block, pl.ds(begin, TBLK), :] = -imag
            other[block, pl.ds(begin + TBLK, TBLK), :] = real

    sides = [plain[r].T for r in range(blocks)]
    for c in range(blocks):
        weights = jnp.concatenate([plain[c], other[c]], axis=1)
        lhs = sides[0] if c == 0 else jnp.concatenate(sides[: c + 1], axis=0)
        both = jnp.dot(lhs, weights, preferred_element_type=jnp.float32)
        row_gain = row_ref[c : c + 1, :]
        for r in range(c + 1):
            pair = r * blocks - r * (r - 1) // 2 + (c - r)
            gain = columns[r * BLK : (r + 1) * BLK, :] * (row_gain * (1.0 / (freq * steps * TBLK)))
            for part in range(2):
                piece = both[r * BLK : (r + 1) * BLK, part * BLK : (part + 1) * BLK]
                out_ref[0, part, pair] = (piece * gain).astype(jnp.bfloat16)


def correlated(name, me, messages, gains, first, count, place, width, before=None):
    parts = len(messages)
    steps = messages[0].shape[0]
    blocks = INPUTS // BLK
    pairs = blocks * (blocks + 1) // 2
    span = parts // blocks * steps * 2 * TBLK
    in_specs = [
        pl.BlockSpec((steps, 1, 2 * TBLK, BLK), lambda i, me: (0, first + i, 0, 0))
        for _ in range(parts)
    ] + [pl.BlockSpec((blocks, BLK), lambda i, me: (0, 0))]
    operands = [me, *messages, gains]
    aliases = {}
    if before is not None:
        aliases[len(operands)] = 0
        in_specs.append(pl.BlockSpec(memory_space=pl.ANY))
        operands.append(before)

    def kernel(me_ref, *refs):
        correlate_kernel(parts, steps, me_ref, *refs)

    return pl.pallas_call(
        kernel,
        name=name,
        grid_spec=pltpu.PrefetchScalarGridSpec(
            num_scalar_prefetch=1,
            grid=(count,),
            in_specs=in_specs,
            out_specs=[
                pl.BlockSpec(
                    (1, 2, pairs, BLK, BLK), lambda i, me: (place + 2 * i, 0, 0, 0, 0)
                ),
                pl.BlockSpec((8, BLK), lambda i, me: (0, 0)),
            ],
            scratch_shapes=[
                pltpu.VMEM((blocks, span, BLK), jnp.bfloat16),
                pltpu.VMEM((blocks, span, BLK), jnp.bfloat16),
                pltpu.VMEM((INPUTS, BLK), jnp.float32),
            ],
        ),
        out_shape=[
            jax.ShapeDtypeStruct((width, 2, pairs, BLK, BLK), jnp.bfloat16),
            jax.ShapeDtypeStruct((8, BLK), jnp.float32),
        ],
        input_output_aliases=aliases,
        compiler_params=pltpu.CompilerParams(vmem_limit_bytes=24 * 2**20),
    )(*operands)


def nothing_kernel(*refs):
    del refs


def gated(name, messages, after):
    spec = pl.BlockSpec(memory_space=pl.ANY)
    return pl.pallas_call(
        nothing_kernel,
        name=name,
        in_specs=[spec] * (len(messages) + len(after)),
        out_specs=[spec] * len(messages),
        out_shape=[jax.ShapeDtypeStruct(m.shape, m.dtype) for m in messages],
        input_output_aliases={i: i for i in range(len(messages))},
    )(*messages, *after)


def per_device(voltages, coeffs):
    freq_count = lax.axis_size("freq")
    parts = lax.axis_size("inp") * freq_count
    inputs, frames, _ = voltages.shape
    width = CH // parts
    fits = (
        inputs == BLK
        and frames == 2 * TBLK
        and TBLK % TAPS == 0
        and parts & (parts - 1) == 0
        and parts >= 16
        and width % 16 == 0
        and parts * BLK == INPUTS * freq_count
        and freq_count * frames * 2 == LANES
    )
    if not fits:
        return any_sizes(voltages, coeffs)
    axes = ("inp", "freq")
    me = lax.axis_index("inp") * freq_count + lax.axis_index("freq")
    me = me.astype(jnp.int32).reshape(1)
    history = passed_along(last_frames(voltages), "freq", 1)
    late = filtered_frames(1, voltages, coeffs)
    early = filtered_frames(0, voltages, coeffs, history)
    tables = parity_tables(parts, width)

    far, near = list(range(parts // 2, parts)), list(range(1, parts // 2))
    order = [s for pair in zip(far, near + [0]) for s in pair if s > 0]

    def send(message, s):
        return lax.ppermute(message, axes, [(i, i ^ s) for i in range(parts)])

    class Chunk:
        def __init__(self, name, messages):
            self.name = name
            self.messages = messages
            self.arrived = {0: messages[0]}
            self.sent = 0

        def go(self, count, after=()):
            which = order[self.sent : self.sent + count]
            chosen = [self.messages[s] for s in which]
            if after:
                chosen = gated(f"gate_{self.name}_{self.sent}", chosen, list(after))
            for s, message in zip(which, chosen):
                self.arrived[s] = send(message, s)
            self.sent += len(which)

        def all(self):
            return [self.arrived[s] for s in range(parts)]

    half = width // 2
    quarter = half // 2
    piece = half // 4
    sets, squares = transformed("spectra_even", parts, me, late[0], early[0], tables[0], [(0, half)])
    first = Chunk("a", sets[0])
    first.go(5)
    sets, more = transformed(
        "spectra_odd",
        parts,
        me,
        late[1],
        early[1],
        tables[1],
        [(0, quarter), (quarter, quarter)],
    )
    second, third = Chunk("b", sets[0]), Chunk("c", sets[1])
    shared = lax.all_gather(jnp.sum(squares + more, axis=0), axes)
    shared = jnp.sum(shared.reshape(parts // freq_count, freq_count, BLK), axis=1)
    gains = 1.0 / jnp.sqrt(shared / (frames * freq_count * CH) + 1e-06)
    first.go(len(order) - 5, [gains])
    second.go(5, [first.arrived[order[9]]])
    out = None
    for step, count in enumerate((3, 3, 4, 0)):
        out, token = correlated(
            f"correlate_a{step}", me, first.all(), gains, step * piece, piece, 2 * step * piece, width, out
        )
        second.go(count, [token]) if count else third.go(4, [token])
    for step, count in enumerate((4, len(order) - 8)):
        out, token = correlated(
            f"correlate_b{step}", me, second.all(), gains, step * piece, piece, 2 * step * piece + 1, width, out
        )
        third.go(count, [token])
    out, _ = correlated(
        "correlate_c", me, third.all(), gains, 0, quarter, 2 * quarter + 1, width, out
    )
    return out


def solution(mesh):
    in_specs = (P(("grp", "inp"), "freq", None), P())
    out_specs = P(("grp", "inp", "freq"), None, None, None, None)
    return jax.shard_map(
        per_device, mesh=mesh, in_specs=in_specs, out_specs=out_specs, check_vma=False
    )
```

```python
import math

import jax
import jax.numpy as jnp
import ml_dtypes
import numpy as np
from jax import lax
from jax.experimental import pallas as pl
from jax.experimental.pallas import tpu as pltpu
from jax.sharding import PartitionSpec as P

SPF = 2048
TAPS = 8
CH = 512
CH0 = 256
INPUTS = 1024
BLK = 128
LANES = 128
UBLK = 16
TBLK = 16
FLIGHT = 5
PITCH = TBLK + 1


def passed_along(x, axis, by):
    length = lax.axis_size(axis)
    pairs = [(i, i + by) for i in range(length) if 0 <= i + by < length]
    return lax.ppermute(x, axis, pairs)


def make_table():
    sample = jnp.arange(SPF, dtype=jnp.int32)[:, None]
    channel = jnp.arange(CH, dtype=jnp.int32)[None, :] + CH0
    phase = sample * channel % SPF
    angle = phase.astype(jnp.float32) * (2.0 * math.pi / SPF)
    return jnp.concatenate([jnp.cos(angle), -jnp.sin(angle)], axis=1).astype(jnp.bfloat16)


def any_sizes(voltages, coeffs):
    inputs_here = voltages.shape[0]
    frames_here = voltages.shape[1]
    inp_count = lax.axis_size("inp")
    freq_count = lax.axis_size("freq")
    frames_all = frames_here * freq_count
    history = voltages[:, frames_here - (TAPS - 1) :, :].astype(jnp.bfloat16)
    earlier = passed_along(history, "freq", 1)
    extended = jnp.concatenate([earlier.astype(jnp.float32), voltages.astype(jnp.float32)], axis=1)
    weights = coeffs.astype(jnp.float32)
    summed = jnp.zeros((inputs_here, frames_here, SPF), jnp.float32)
    for tap_index in range(TAPS):
        begin = TAPS - 1 - tap_index
        summed = summed + weights[tap_index] * extended[:, begin : begin + frames_here, :]
    filtered = summed.astype(jnp.bfloat16).reshape(inputs_here * frames_here, SPF)
    spectrum_t = jnp.einsum("nj,rn->jr", make_table(), filtered, preferred_element_type=jnp.float32)
    spectrum_t = spectrum_t.reshape(2 * CH, inputs_here, frames_here)
    squares = jnp.sum(spectrum_t * spectrum_t, axis=(0, 2))
    power = lax.psum(squares, "freq") / (frames_all * CH)
    gains = 1.0 / jnp.sqrt(power + 1e-06)
    scaled = (spectrum_t * gains[None, :, None]).astype(jnp.bfloat16)
    scaled = scaled.reshape(2, CH, inputs_here * frames_here)
    arrived = lax.all_to_all(scaled[None], ("inp", "freq"), split_axis=2, concat_axis=0, tiled=True)
    width_here = arrived.shape[-2]
    arranged = arrived.reshape(inp_count, freq_count, 2, width_here, inputs_here, frames_here)
    arranged = jnp.transpose(arranged, (3, 0, 4, 2, 1, 5))
    stacked = arranged.reshape(width_here, INPUTS, 2 * frames_all)
    other = jnp.concatenate([-stacked[:, :, frames_all:], stacked[:, :, :frames_all]], axis=2)
    block_count = INPUTS // BLK
    scale = 1.0 / frames_all
    pieces = []
    for row_index in range(block_count):
        row_panel = stacked[:, row_index * BLK : (row_index + 1) * BLK]
        real_part = jnp.einsum(
            "cut,cmt->cum",
            row_panel,
            stacked[:, row_index * BLK :],
            preferred_element_type=jnp.float32,
        )
        imag_part = jnp.einsum(
            "cut,cmt->cum",
            row_panel,
            other[:, row_index * BLK :],
            preferred_element_type=jnp.float32,
        )
        band = jnp.stack([real_part, imag_part], axis=1) * scale
        for col_index in range(row_index, block_count):
            begin = (col_index - row_index) * BLK
            pieces.append(band[:, :, :, begin : begin + BLK])
    return jnp.stack(pieces, axis=2).astype(jnp.bfloat16)


def turned_over(rows):
    rows = list(rows)
    place = lax.broadcasted_iota(jnp.int32, (8, LANES), 0)
    for shift in (4, 2, 1):
        low = jnp.bitwise_and(place, shift) == 0
        for i in range(8):
            if i & shift == 0:
                near, far = rows[i], rows[i + shift]
                rows[i] = jnp.where(low, near, pltpu.roll(far, shift, 0))
                rows[i + shift] = jnp.where(low, pltpu.roll(near, 8 - shift, 0), far)
    return rows


def frames_of(v_ref, cols):
    groups = []
    for group in range(UBLK // 8):
        groups.append(turned_over([v_ref[group * 8 + i, :, cols] for i in range(8)]))
    return [[group[t].astype(jnp.float32) for group in groups] for t in range(8)]


def history_kernel(v_ref, *refs):
    out_ref = refs[-1]

    def column(step, carry):
        cols = pl.ds(pl.multiple_of(step * LANES, LANES), LANES)
        for t, frame in enumerate(frames_of(v_ref, cols)):
            out_ref[t, :, cols] = jnp.concatenate(frame, axis=0).astype(jnp.bfloat16)
        return carry

    lax.fori_loop(0, SPF // LANES, column, 0)


def last_frames(voltages, after):
    inputs, frames, _ = voltages.shape
    last = frames // TAPS - 1
    return pl.pallas_call(
        history_kernel,
        name="history",
        grid=(inputs // UBLK,),
        in_specs=[pl.BlockSpec((UBLK, TAPS, SPF), lambda i: (i, last, 0))]
        + [pl.BlockSpec(memory_space=pl.ANY)] * len(after),
        out_specs=pl.BlockSpec((TAPS, UBLK, SPF), lambda i: (0, i, 0)),
        out_shape=jax.ShapeDtypeStruct((TAPS, inputs, SPF), jnp.bfloat16),
    )(voltages, *after)


def parity_tables(parts, width):
    tables = []
    for parity in range(2):
        within = np.arange(parity, width, 2)
        channel = (np.arange(parts)[:, None] * width + within[None, :]).reshape(-1) + CH0
        phase = channel[:, None].astype(np.int64) * np.arange(SPF // 2)[None, :] % SPF
        angle = phase.astype(np.float32) * np.float32(2.0 * math.pi / SPF)
        wide = angle.astype(np.float64)
        both = np.stack([np.cos(wide), -np.sin(wide)], axis=1)
        both = both.reshape(-1, SPF // 2).astype(np.float32)
        tables.append(jnp.asarray(both.astype(ml_dtypes.bfloat16)))
    return tables


def filter_step(block, sources, c_ref, even, odd):
    half = SPF // 2
    groups = UBLK // 8
    here = pl.ds(pl.multiple_of(pl.program_id(0) * UBLK, UBLK), UBLK)

    def column(step, carry):
        sides = []
        before = []
        for side in range(2):
            cols = pl.ds(pl.multiple_of(step * LANES + side * half, LANES), LANES)
            weights = c_ref[:, cols].astype(jnp.float32)
            taps = [jnp.broadcast_to(weights[k : k + 1], (8, LANES)) for k in range(TAPS)]
            sides.append((cols, taps))
            if block == 0:
                wide = [sources[0][t, :, cols].astype(jnp.float32) for t in range(TAPS)]
                before.append([[w[g * 8 : (g + 1) * 8] for g in range(groups)] for w in wide])
            else:
                before.append(frames_of(sources[0], cols))
        out = pl.ds(pl.multiple_of(step * LANES, LANES), LANES)
        for part in range(TBLK // TAPS):
            made = []
            for side, (cols, taps) in enumerate(sides):
                now = frames_of(sources[1 + part], cols)
                window = before[side] + now
                before[side] = now
                totals = []
                for t in range(TAPS):
                    frame = []
                    for g in range(groups):
                        total = taps[0] * window[TAPS + t][g]
                        for k in range(1, TAPS):
                            total = total + taps[k] * window[TAPS + t - k][g]
                        frame.append(total)
                    totals.append(jnp.concatenate(frame, axis=0))
                made.append(totals)
            for t in range(TAPS):
                at = part * TAPS + t
                even[at, here, out] = (made[0][t] + made[1][t]).astype(jnp.bfloat16)
                odd[at, here, out] = (made[0][t] - made[1][t]).astype(jnp.bfloat16)
        return carry

    lax.fori_loop(0, half // LANES, column, 0)


def front_kernel(block, parts, where, me_ref, *refs):
    count = 1 + TBLK // TAPS
    sources, c_ref, tables = refs[:count], refs[count], refs[count + 1 : count + 3]
    earlier_ref = refs[count + 3] if block == 0 else None
    outs = refs[count + (4 if block == 0 else 3) : -4]
    power_ref, even, odd, turned = refs[-4:]
    filter_step(block, sources, c_ref, even, odd)

    @pl.when(pl.program_id(0) == pl.num_programs(0) - 1)
    def _():
        me = me_ref[0]
        square = jnp.zeros((8, BLK), jnp.float32)
        for parity, filtered in enumerate((even, odd)):
            rows = tables[parity].shape[0]
            own = rows // parts
            spectrum = lax.dot_general(
                tables[parity][...],
                filtered[...].reshape(-1, SPF // 2),
                (((1,), (1,)), ((), ())),
                preferred_element_type=jnp.float32,
            )
            for t in range(TBLK):
                frame = spectrum[:, t * BLK : (t + 1) * BLK]
                turned[pl.ds(t, rows, stride=PITCH), :] = frame
                square = square + jnp.sum((frame * frame).reshape(rows // 8, 8, BLK), axis=0)
            for s in range(parts):
                begin = jnp.bitwise_xor(me, s) * (own * PITCH)
                for channel in range(own // 2):
                    index, place = where(s, parity, channel)
                    for half in range(2):
                        row = channel * 2 + half
                        value = turned[pl.ds(begin + row * PITCH, TBLK), :].astype(jnp.bfloat16)
                        to = (place * 2 + half) * TBLK
                        outs[index][to : to + TBLK, :] = value
        if block == 0:
            square = square + earlier_ref[...]
            rest = jnp.sum(square, axis=0, keepdims=True)
            terms = []
            for _ in range(3):
                term = rest.astype(jnp.bfloat16).astype(jnp.float32)
                terms.append(term)
                rest = rest - term
            terms.append(jnp.zeros((TBLK - 3, BLK), jnp.float32))
            tail = jnp.concatenate(terms, axis=0).astype(jnp.bfloat16)
            for s in range(parts):
                size = outs[s].shape[0]
                outs[s][size - TBLK :, :] = tail
        power_ref[...] = square


def front(block, parts, me, voltages, coeffs, tables, shapes, where, history=None, earlier=None):
    inputs, frames, _ = voltages.shape
    half = SPF // 2
    first = block * (TBLK // TAPS)
    in_specs, operands = [], []
    for place in range(first - 1, first + TBLK // TAPS):
        if place < 0:
            in_specs.append(pl.BlockSpec((TAPS, UBLK, SPF), lambda i, me: (0, i, 0)))
            operands.append(history)
        else:
            in_specs.append(
                pl.BlockSpec((UBLK, TAPS, SPF), lambda i, me, place=place: (i, place, 0))
            )
            operands.append(voltages)
    operands += [coeffs, *tables]
    if block == 0:
        operands.append(earlier)
    for array in operands[len(in_specs) :]:
        in_specs.append(pl.BlockSpec(array.shape, lambda i, me: (0, 0)))
    shapes = [jax.ShapeDtypeStruct(shape, jnp.bfloat16) for shape in shapes]
    shapes.append(jax.ShapeDtypeStruct((8, BLK), jnp.float32))

    def kernel(me_ref, *refs):
        front_kernel(block, parts, where, me_ref, *refs)

    return pl.pallas_call(
        kernel,
        name=f"front_{block}",
        grid_spec=pltpu.PrefetchScalarGridSpec(
            num_scalar_prefetch=1,
            grid=(inputs // UBLK,),
            in_specs=in_specs,
            out_specs=[pl.BlockSpec(shape.shape, lambda i, me: (0, 0)) for shape in shapes],
            scratch_shapes=[
                pltpu.VMEM((TBLK, inputs, half), jnp.bfloat16),
                pltpu.VMEM((TBLK, inputs, half), jnp.bfloat16),
                pltpu.VMEM((tables[0].shape[0] * PITCH + 8, BLK), jnp.float32),
            ],
        ),
        out_shape=shapes,
        compiler_params=pltpu.CompilerParams(vmem_limit_bytes=50 * 2**20),
    )(me, *operands)


def correlate_kernel(parts, me_ref, *refs):
    late, early, powers = refs[:parts], refs[parts : 2 * parts], refs[2 * parts : 3 * parts]
    out_ref, token_ref, plain, other, columns, lines, shares = refs[-7:]
    blocks = INPUTS // BLK
    freq = parts // blocks
    me = me_ref[0]

    @pl.when(pl.program_id(0) == 0)
    def _():
        token_ref[...] = jnp.zeros_like(token_ref)
        for s in range(parts):
            terms = powers[s][...].astype(jnp.float32)
            power = terms[0:1] + terms[1:2] + terms[2:3]
            shares[jnp.bitwise_xor(me, s)] = jnp.broadcast_to(power, (8, BLK))
        for r in range(blocks):
            power = shares[r * freq]
            for f in range(1, freq):
                power = power + shares[r * freq + f]
            gain = 1.0 / jnp.sqrt(power / (freq * 2 * TBLK * CH) + 1e-06)
            lines[r] = gain
            columns[r * BLK : (r + 1) * BLK, :] = jnp.broadcast_to(gain[0:1], (BLK, BLK)).T

    for s in range(parts):
        source = jnp.bitwise_xor(me, s)
        block, place = source // freq, source % freq
        for half, ref in enumerate((late[s], early[s])):
            begin = pl.multiple_of((place * 2 + half) * 2 * TBLK, 2 * TBLK)
            real = ref[:TBLK, :]
            imag = ref[TBLK:, :]
            plain[block, pl.ds(begin, TBLK), :] = real
            plain[block, pl.ds(begin + TBLK, TBLK), :] = imag
            other[block, pl.ds(begin, TBLK), :] = -imag
            other[block, pl.ds(begin + TBLK, TBLK), :] = real

    sides = [plain[r].T for r in range(blocks)]
    for c in range(blocks):
        weights = jnp.concatenate([plain[c], other[c]], axis=1)
        line = lines[c][0:1] * (1.0 / (freq * 2 * TBLK))
        for r in range(c + 1):
            both = jnp.dot(sides[r], weights, preferred_element_type=jnp.float32)
            pair = r * blocks - r * (r - 1) // 2 + (c - r)
            gain = columns[r * BLK : (r + 1) * BLK, :] * line
            for part in range(2):
                piece = both[:, part * BLK : (part + 1) * BLK]
                out_ref[0, part, pair] = (piece * gain).astype(jnp.bfloat16)


def correlated(name, me, late, early, powers, spot, count, place, width, before, after=()):
    parts = len(late)
    blocks = INPUTS // BLK
    pairs = blocks * (blocks + 1) // 2
    span = parts // blocks * 4 * TBLK
    first, second = spot
    last = powers[0].shape[0] // TBLK - 1
    in_specs = (
        [pl.BlockSpec((2 * TBLK, BLK), lambda i, me: (first + i, 0))] * parts
        + [pl.BlockSpec((2 * TBLK, BLK), lambda i, me: (second + i, 0))] * parts
        + [pl.BlockSpec((TBLK, BLK), lambda i, me: (last, 0))] * parts
    )
    operands = [me, *late, *early, *powers]
    aliases = {}
    if before is not None:
        aliases[len(operands)] = 0
        operands.append(before)
    operands += list(after)
    in_specs += [pl.BlockSpec(memory_space=pl.ANY)] * (len(operands) - 1 - len(in_specs))

    def kernel(me_ref, *refs):
        correlate_kernel(parts, me_ref, *refs)

    return pl.pallas_call(
        kernel,
        name=name,
        grid_spec=pltpu.PrefetchScalarGridSpec(
            num_scalar_prefetch=1,
            grid=(count,),
            in_specs=in_specs,
            out_specs=[
                pl.BlockSpec(
                    (1, 2, pairs, BLK, BLK), lambda i, me: (place + 2 * i, 0, 0, 0, 0)
                ),
                pl.BlockSpec((8, BLK), lambda i, me: (0, 0)),
            ],
            scratch_shapes=[
                pltpu.VMEM((blocks, span, BLK), jnp.bfloat16),
                pltpu.VMEM((blocks, span, BLK), jnp.bfloat16),
                pltpu.VMEM((INPUTS, BLK), jnp.float32),
                pltpu.VMEM((blocks, 8, BLK), jnp.float32),
                pltpu.VMEM((parts, 8, BLK), jnp.float32),
            ],
        ),
        out_shape=[
            jax.ShapeDtypeStruct((width, 2, pairs, BLK, BLK), jnp.bfloat16),
            jax.ShapeDtypeStruct((8, BLK), jnp.float32),
        ],
        input_output_aliases=aliases,
        compiler_params=pltpu.CompilerParams(vmem_limit_bytes=24 * 2**20),
    )(*operands)


def nothing_kernel(*refs):
    del refs


def gated(name, messages, after):
    spec = pl.BlockSpec(memory_space=pl.ANY)
    return pl.pallas_call(
        nothing_kernel,
        name=name,
        in_specs=[spec] * (len(messages) + len(after)),
        out_specs=[spec] * len(messages),
        out_shape=[jax.ShapeDtypeStruct(m.shape, m.dtype) for m in messages],
        input_output_aliases={i: i for i in range(len(messages))},
    )(*messages, *after)


def per_device(voltages, coeffs):
    freq_count = lax.axis_size("freq")
    parts = lax.axis_size("inp") * freq_count
    inputs, frames, _ = voltages.shape
    width = CH // parts
    fits = (
        inputs == BLK
        and frames == 2 * TBLK
        and TBLK % TAPS == 0
        and parts & (parts - 1) == 0
        and parts >= 16
        and width % 16 == 0
        and parts * BLK == INPUTS * freq_count
        and freq_count * frames * 2 == LANES
    )
    if not fits:
        return any_sizes(voltages, coeffs)
    axes = ("inp", "freq")
    me = lax.axis_index("inp") * freq_count + lax.axis_index("freq")
    me = me.astype(jnp.int32).reshape(1)
    half = width // 2
    extra = half // 4
    tables = parity_tables(parts, width)

    far, near = list(range(parts // 2, parts)), list(range(1, parts // 2))
    far = [s for pair in zip(far[: parts // 4], far[parts // 4 :]) for s in pair]
    log = []

    def send(name, messages, order, arrived, after=()):
        for s in order:
            waits = list(after) + (log[-FLIGHT:][:1] if len(log) >= FLIGHT else [])
            message = messages[s]
            if waits:
                (message,) = gated(f"gate_{name}_{s}", [message], waits)
            arrived[s] = lax.ppermute(message, axes, [(i, i ^ s) for i in range(parts)])
            log.append(arrived[s])

    def mixed(some_far, some_near):
        out = []
        while some_far or some_near:
            out += some_far[:2] + some_near[:1] if some_far else some_near
            some_near = some_near[1:] if some_far else []
            some_far = some_far[2:]
        return out

    made = front(
        1,
        parts,
        me,
        voltages,
        coeffs,
        tables,
        [(width * 2 * TBLK, BLK)] * parts,
        lambda s, parity, channel: (s, parity * half + channel),
    )
    late, earlier = {0: made[0]}, made[parts]
    ahead = FLIGHT - 1
    send("late", made, near[:1] + far[:ahead], late)

    history = passed_along(last_frames(voltages, [late[1]]), "freq", 1)
    made_early = front(
        0,
        parts,
        me,
        voltages,
        coeffs,
        tables,
        [((half + extra) * 2 * TBLK + TBLK, BLK)] * parts + [((half - extra) * 2 * TBLK, BLK)] * parts,
        lambda s, parity, channel: (
            (s, parity * half + channel)
            if parity == 0 or channel < extra
            else (parts + s, channel - extra)
        ),
        history,
        earlier,
    )
    send("late", made, mixed(far[ahead:], near[1:]), late, [made_early[-1]])
    one, two = made_early[:parts], made_early[parts : 2 * parts]
    early, rest = {0: one[0]}, {0: two[0]}
    send("one", one, mixed(far, near), early)

    def every(found):
        return [found[s] for s in range(parts)]

    send("two", two, far[:FLIGHT], rest)
    late, early = every(late), every(early)
    left_far, left_near = far[FLIGHT:], list(near)
    out, after = None, []
    pieces = [(parity, i) for parity, size in ((0, half), (1, extra)) for i in range(0, size, extra)]
    for parity, i in pieces:
        spot = (parity * half + i, parity * half + i)
        out, token = correlated(
            f"correlate_{parity}_{i}", me, late, early, early, spot, extra, 2 * i + parity, width, out, after
        )
        final = (parity, i) == pieces[-1]
        now = left_near if final else left_near[:1]
        send("two", two, now + left_far[: len(left_far) if final else 1], rest, [token])
        after = [rest[now[0]]] if now else []
        left_near, left_far = left_near[1:], left_far[1:]
    out, _ = correlated(
        "correlate_rest",
        me,
        late,
        every(rest),
        early,
        (half + extra, 0),
        half - extra,
        2 * extra + 1,
        width,
        out,
    )
    return out


def solution(mesh):
    in_specs = (P(("grp", "inp"), "freq", None), P())
    out_specs = P(("grp", "inp", "freq"), None, None, None, None)
    return jax.shard_map(
        per_device, mesh=mesh, in_specs=in_specs, out_specs=out_specs, check_vma=False
    )
```

```python
import math

import jax
import jax.numpy as jnp
import ml_dtypes
import numpy as np
from jax import lax
from jax.experimental import pallas as pl
from jax.experimental.pallas import tpu as pltpu
from jax.sharding import PartitionSpec as P

SPF = 2048
TAPS = 8
CH = 512
CH0 = 256
INPUTS = 1024
BLK = 128
LANES = 128
UBLK = 16
TBLK = 16
VMEM_BYTES = 64 * 2**20 - 2**16
FLIGHT = 5
PITCH = TBLK + 1


def passed_along(x, axis, by):
    length = lax.axis_size(axis)
    pairs = [(i, i + by) for i in range(length) if 0 <= i + by < length]
    return lax.ppermute(x, axis, pairs)


def make_table():
    sample = jnp.arange(SPF, dtype=jnp.int32)[:, None]
    channel = jnp.arange(CH, dtype=jnp.int32)[None, :] + CH0
    phase = sample * channel % SPF
    angle = phase.astype(jnp.float32) * (2.0 * math.pi / SPF)
    return jnp.concatenate([jnp.cos(angle), -jnp.sin(angle)], axis=1).astype(jnp.bfloat16)


def any_sizes(voltages, coeffs):
    inputs_here = voltages.shape[0]
    frames_here = voltages.shape[1]
    inp_count = lax.axis_size("inp")
    freq_count = lax.axis_size("freq")
    frames_all = frames_here * freq_count
    history = voltages[:, frames_here - (TAPS - 1) :, :].astype(jnp.bfloat16)
    earlier = passed_along(history, "freq", 1)
    extended = jnp.concatenate([earlier.astype(jnp.float32), voltages.astype(jnp.float32)], axis=1)
    weights = coeffs.astype(jnp.float32)
    summed = jnp.zeros((inputs_here, frames_here, SPF), jnp.float32)
    for tap_index in range(TAPS):
        begin = TAPS - 1 - tap_index
        summed = summed + weights[tap_index] * extended[:, begin : begin + frames_here, :]
    filtered = summed.astype(jnp.bfloat16).reshape(inputs_here * frames_here, SPF)
    spectrum_t = jnp.einsum("nj,rn->jr", make_table(), filtered, preferred_element_type=jnp.float32)
    spectrum_t = spectrum_t.reshape(2 * CH, inputs_here, frames_here)
    squares = jnp.sum(spectrum_t * spectrum_t, axis=(0, 2))
    power = lax.psum(squares, "freq") / (frames_all * CH)
    gains = 1.0 / jnp.sqrt(power + 1e-06)
    scaled = (spectrum_t * gains[None, :, None]).astype(jnp.bfloat16)
    scaled = scaled.reshape(2, CH, inputs_here * frames_here)
    arrived = lax.all_to_all(scaled[None], ("inp", "freq"), split_axis=2, concat_axis=0, tiled=True)
    width_here = arrived.shape[-2]
    arranged = arrived.reshape(inp_count, freq_count, 2, width_here, inputs_here, frames_here)
    arranged = jnp.transpose(arranged, (3, 0, 4, 2, 1, 5))
    stacked = arranged.reshape(width_here, INPUTS, 2 * frames_all)
    other = jnp.concatenate([-stacked[:, :, frames_all:], stacked[:, :, :frames_all]], axis=2)
    block_count = INPUTS // BLK
    scale = 1.0 / frames_all
    pieces = []
    for row_index in range(block_count):
        row_panel = stacked[:, row_index * BLK : (row_index + 1) * BLK]
        real_part = jnp.einsum(
            "cut,cmt->cum",
            row_panel,
            stacked[:, row_index * BLK :],
            preferred_element_type=jnp.float32,
        )
        imag_part = jnp.einsum(
            "cut,cmt->cum",
            row_panel,
            other[:, row_index * BLK :],
            preferred_element_type=jnp.float32,
        )
        band = jnp.stack([real_part, imag_part], axis=1) * scale
        for col_index in range(row_index, block_count):
            begin = (col_index - row_index) * BLK
            pieces.append(band[:, :, :, begin : begin + BLK])
    return jnp.stack(pieces, axis=2).astype(jnp.bfloat16)


def turned_over(rows):
    rows = list(rows)
    place = lax.broadcasted_iota(jnp.int32, (8, LANES), 0)
    for shift in (4, 2, 1):
        low = jnp.bitwise_and(place, shift) == 0
        for i in range(8):
            if i & shift == 0:
                near, far = rows[i], rows[i + shift]
                rows[i] = jnp.where(low, near, pltpu.roll(far, shift, 0))
                rows[i + shift] = jnp.where(low, pltpu.roll(near, 8 - shift, 0), far)
    return rows


def frames_of(v_ref, cols):
    groups = []
    for group in range(UBLK // 8):
        groups.append(turned_over([v_ref[group * 8 + i, :, cols] for i in range(8)]))
    return [[group[t].astype(jnp.float32) for group in groups] for t in range(8)]


def kept(array):
    return pltpu.with_memory_space_constraint(array, pltpu.HBM)


def parity_tables(parts, width):
    tables = []
    for parity in range(2):
        within = np.arange(parity, width, 2)
        channel = (np.arange(parts)[:, None] * width + within[None, :]).reshape(-1) + CH0
        phase = channel[:, None].astype(np.int64) * np.arange(SPF // 2)[None, :] % SPF
        angle = phase.astype(np.float32) * np.float32(2.0 * math.pi / SPF)
        wide = angle.astype(np.float64)
        both = np.stack([np.cos(wide), -np.sin(wide)], axis=1)
        both = both.reshape(-1, SPF // 2).astype(np.float32)
        tables.append(jnp.asarray(both.astype(ml_dtypes.bfloat16)))
    return tables


def filter_step(block, sources, c_ref, even, odd, last_ref):
    half = SPF // 2
    groups = UBLK // 8
    here = pl.ds(pl.multiple_of(pl.program_id(0) * UBLK, UBLK), UBLK)

    def column(step, carry):
        sides = []
        before = []
        for side in range(2):
            cols = pl.ds(pl.multiple_of(step * LANES + side * half, LANES), LANES)
            weights = c_ref[:, cols].astype(jnp.float32)
            taps = [jnp.broadcast_to(weights[k : k + 1], (8, LANES)) for k in range(TAPS)]
            sides.append((cols, taps))
            if block == 0:
                wide = [sources[0][t, :, cols].astype(jnp.float32) for t in range(TAPS)]
                before.append([[w[g * 8 : (g + 1) * 8] for g in range(groups)] for w in wide])
            else:
                before.append(frames_of(sources[0], cols))
        out = pl.ds(pl.multiple_of(step * LANES, LANES), LANES)
        for part in range(TBLK // TAPS):
            made = []
            for side, (cols, taps) in enumerate(sides):
                now = frames_of(sources[1 + part], cols)
                window = before[side] + now
                before[side] = now
                totals = []
                for t in range(TAPS):
                    frame = []
                    for g in range(groups):
                        total = taps[0] * window[TAPS + t][g]
                        for k in range(1, TAPS):
                            total = total + taps[k] * window[TAPS + t - k][g]
                        frame.append(total)
                    totals.append(jnp.concatenate(frame, axis=0))
                made.append(totals)
                if last_ref is not None and part == TBLK // TAPS - 1:
                    for t in range(TAPS):
                        frame = jnp.concatenate(now[t], axis=0)
                        last_ref[t, :, cols] = frame.astype(jnp.bfloat16)
            for t in range(TAPS):
                at = part * TAPS + t
                even[at, here, out] = (made[0][t] + made[1][t]).astype(jnp.bfloat16)
                odd[at, here, out] = (made[0][t] - made[1][t]).astype(jnp.bfloat16)
        return carry

    lax.fori_loop(0, half // LANES, column, 0)


def front_kernel(block, parts, where, me_ref, *refs):
    count = 1 + TBLK // TAPS
    sources, c_ref, tables = refs[:count], refs[count], refs[count + 1 : count + 3]
    earlier_ref = refs[count + 3] if block == 0 else None
    outs = refs[count + (4 if block == 0 else 3) : -4]
    last_ref = None if block == 0 else outs[-1]
    power_ref, even, odd, turned = refs[-4:]
    filter_step(block, sources, c_ref, even, odd, last_ref)

    @pl.when(pl.program_id(0) == pl.num_programs(0) - 1)
    def _():
        me = me_ref[0]
        square = jnp.zeros((8, BLK), jnp.float32)
        for parity, filtered in enumerate((even, odd)):
            rows = tables[parity].shape[0]
            own = rows // parts
            spectrum = lax.dot_general(
                tables[parity][...],
                filtered[...].reshape(-1, SPF // 2),
                (((1,), (1,)), ((), ())),
                preferred_element_type=jnp.float32,
            )
            for t in range(TBLK):
                frame = spectrum[:, t * BLK : (t + 1) * BLK]
                turned[pl.ds(t, rows, stride=PITCH), :] = frame
                square = square + jnp.sum((frame * frame).reshape(rows // 8, 8, BLK), axis=0)
            for s in range(parts):
                begin = jnp.bitwise_xor(me, s) * (own * PITCH)
                for channel in range(own // 2):
                    index, place = where(s, parity, channel)
                    for half in range(2):
                        row = channel * 2 + half
                        value = turned[pl.ds(begin + row * PITCH, TBLK), :].astype(jnp.bfloat16)
                        to = (place * 2 + half) * TBLK
                        outs[index][to : to + TBLK, :] = value
        if block == 0:
            square = square + earlier_ref[...]
            rest = jnp.sum(square, axis=0, keepdims=True)
            terms = []
            for _ in range(3):
                term = rest.astype(jnp.bfloat16).astype(jnp.float32)
                terms.append(term)
                rest = rest - term
            terms.append(jnp.zeros((TBLK - 3, BLK), jnp.float32))
            tail = jnp.concatenate(terms, axis=0).astype(jnp.bfloat16)
            for s in range(parts):
                size = outs[s].shape[0]
                outs[s][size - TBLK :, :] = tail
        power_ref[...] = square


def front(block, parts, me, voltages, coeffs, tables, shapes, where, history=None, earlier=None):
    inputs, frames, _ = voltages.shape
    half = SPF // 2
    first = block * (TBLK // TAPS)
    in_specs, operands = [], []
    for place in range(first - 1, first + TBLK // TAPS):
        if place < 0:
            in_specs.append(pl.BlockSpec((TAPS, UBLK, SPF), lambda i, me: (0, i, 0)))
            operands.append(kept(history))
        else:
            in_specs.append(
                pl.BlockSpec((UBLK, TAPS, SPF), lambda i, me, place=place: (i, place, 0))
            )
            operands.append(voltages)
    operands += [coeffs, *tables]
    if block == 0:
        operands.append(earlier)
    for array in operands[len(in_specs) :]:
        in_specs.append(pl.BlockSpec(array.shape, lambda i, me: (0, 0)))
    out_shapes = [pltpu.HBM(shape, jnp.bfloat16) for shape in shapes]
    out_specs = [pl.BlockSpec(shape, lambda i, me: (0, 0)) for shape in shapes]
    if block == 1:
        out_shapes.append(pltpu.HBM((TAPS, inputs, SPF), jnp.bfloat16))
        out_specs.append(pl.BlockSpec((TAPS, UBLK, SPF), lambda i, me: (0, i, 0)))
    out_shapes.append(jax.ShapeDtypeStruct((8, BLK), jnp.float32))
    out_specs.append(pl.BlockSpec((8, BLK), lambda i, me: (0, 0)))

    def kernel(me_ref, *refs):
        front_kernel(block, parts, where, me_ref, *refs)

    return pl.pallas_call(
        kernel,
        name=f"front_{block}",
        grid_spec=pltpu.PrefetchScalarGridSpec(
            num_scalar_prefetch=1,
            grid=(inputs // UBLK,),
            in_specs=in_specs,
            out_specs=out_specs,
            scratch_shapes=[
                pltpu.VMEM((TBLK, inputs, half), jnp.bfloat16),
                pltpu.VMEM((TBLK, inputs, half), jnp.bfloat16),
                pltpu.VMEM((tables[0].shape[0] * PITCH + 8, BLK), jnp.float32),
            ],
        ),
        out_shape=out_shapes,
        compiler_params=pltpu.CompilerParams(vmem_limit_bytes=VMEM_BYTES),
    )(me, *operands)


def correlate_kernel(parts, me_ref, *refs):
    late, early, powers = refs[:parts], refs[parts : 2 * parts], refs[2 * parts : 3 * parts]
    out_ref, token_ref, plain, other, columns, lines, shares = refs[-7:]
    blocks = INPUTS // BLK
    freq = parts // blocks
    me = me_ref[0]

    @pl.when(pl.program_id(0) == 0)
    def _():
        token_ref[...] = jnp.zeros_like(token_ref)
        for s in range(parts):
            terms = powers[s][...].astype(jnp.float32)
            power = terms[0:1] + terms[1:2] + terms[2:3]
            shares[jnp.bitwise_xor(me, s)] = jnp.broadcast_to(power, (8, BLK))
        for r in range(blocks):
            power = shares[r * freq]
            for f in range(1, freq):
                power = power + shares[r * freq + f]
            gain = 1.0 / jnp.sqrt(power / (freq * 2 * TBLK * CH) + 1e-06)
            lines[r] = gain
            columns[r * BLK : (r + 1) * BLK, :] = jnp.broadcast_to(gain[0:1], (BLK, BLK)).T

    for s in range(parts):
        source = jnp.bitwise_xor(me, s)
        block, place = source // freq, source % freq
        for half, ref in enumerate((late[s], early[s])):
            begin = pl.multiple_of((place * 2 + half) * 2 * TBLK, 2 * TBLK)
            real = ref[:TBLK, :]
            imag = ref[TBLK:, :]
            plain[block, pl.ds(begin, TBLK), :] = real
            plain[block, pl.ds(begin + TBLK, TBLK), :] = imag
            other[block, pl.ds(begin, TBLK), :] = -imag
            other[block, pl.ds(begin + TBLK, TBLK), :] = real

    sides = [plain[r].T for r in range(blocks)]
    for c in range(blocks):
        weights = jnp.concatenate([plain[c], other[c]], axis=1)
        line = lines[c][0:1] * (1.0 / (freq * 2 * TBLK))
        for r in range(c + 1):
            both = jnp.dot(sides[r], weights, preferred_element_type=jnp.float32)
            pair = r * blocks - r * (r - 1) // 2 + (c - r)
            gain = columns[r * BLK : (r + 1) * BLK, :] * line
            for part in range(2):
                piece = both[:, part * BLK : (part + 1) * BLK]
                out_ref[0, part, pair] = (piece * gain).astype(jnp.bfloat16)


def correlated(name, me, late, early, powers, spot, count, place, width, before, after=()):
    parts = len(late)
    blocks = INPUTS // BLK
    pairs = blocks * (blocks + 1) // 2
    span = parts // blocks * 4 * TBLK
    first, second = spot
    last = powers[0].shape[0] // TBLK - 1
    in_specs = (
        [pl.BlockSpec((2 * TBLK, BLK), lambda i, me: (first + i, 0))] * parts
        + [pl.BlockSpec((2 * TBLK, BLK), lambda i, me: (second + i, 0))] * parts
        + [pl.BlockSpec((TBLK, BLK), lambda i, me: (last, 0))] * parts
    )
    operands = [me, *map(kept, late), *map(kept, early), *map(kept, powers)]
    aliases = {}
    if before is not None:
        aliases[len(operands)] = 0
        operands.append(before)
    operands += map(kept, after)
    in_specs += [pl.BlockSpec(memory_space=pl.ANY)] * (len(operands) - 1 - len(in_specs))

    def kernel(me_ref, *refs):
        correlate_kernel(parts, me_ref, *refs)

    return pl.pallas_call(
        kernel,
        name=name,
        grid_spec=pltpu.PrefetchScalarGridSpec(
            num_scalar_prefetch=1,
            grid=(count,),
            in_specs=in_specs,
            out_specs=[
                pl.BlockSpec(
                    (1, 2, pairs, BLK, BLK), lambda i, me: (place + 2 * i, 0, 0, 0, 0)
                ),
                pl.BlockSpec((8, BLK), lambda i, me: (0, 0)),
            ],
            scratch_shapes=[
                pltpu.VMEM((blocks, span, BLK), jnp.bfloat16),
                pltpu.VMEM((blocks, span, BLK), jnp.bfloat16),
                pltpu.VMEM((INPUTS, BLK), jnp.float32),
                pltpu.VMEM((blocks, 8, BLK), jnp.float32),
                pltpu.VMEM((parts, 8, BLK), jnp.float32),
            ],
        ),
        out_shape=[
            jax.ShapeDtypeStruct((width, 2, pairs, BLK, BLK), jnp.bfloat16),
            jax.ShapeDtypeStruct((8, BLK), jnp.float32),
        ],
        input_output_aliases=aliases,
        compiler_params=pltpu.CompilerParams(vmem_limit_bytes=VMEM_BYTES),
    )(*operands)


def nothing_kernel(*refs):
    del refs


def gated(name, messages, after):
    spec = pl.BlockSpec(memory_space=pl.ANY)
    return pl.pallas_call(
        nothing_kernel,
        name=name,
        in_specs=[spec] * (len(messages) + len(after)),
        out_specs=[spec] * len(messages),
        out_shape=[pltpu.HBM(m.shape, m.dtype) for m in messages],
        input_output_aliases={i: i for i in range(len(messages))},
        compiler_params=pltpu.CompilerParams(vmem_limit_bytes=VMEM_BYTES),
    )(*map(kept, messages), *map(kept, after))


def per_device(voltages, coeffs):
    freq_count = lax.axis_size("freq")
    parts = lax.axis_size("inp") * freq_count
    inputs, frames, _ = voltages.shape
    width = CH // parts
    fits = (
        inputs == BLK
        and frames == 2 * TBLK
        and TBLK % TAPS == 0
        and parts & (parts - 1) == 0
        and parts >= 16
        and width % 16 == 0
        and parts * BLK == INPUTS * freq_count
        and freq_count * frames * 2 == LANES
    )
    if not fits:
        return any_sizes(voltages, coeffs)
    axes = ("inp", "freq")
    me = lax.axis_index("inp") * freq_count + lax.axis_index("freq")
    me = me.astype(jnp.int32).reshape(1)
    half = width // 2
    extra = half // 4
    tables = parity_tables(parts, width)

    far, near = list(range(parts // 2, parts)), list(range(1, parts // 2))
    far = [s for pair in zip(far[: parts // 4], far[parts // 4 :]) for s in pair]
    log = []

    def send(name, messages, order, arrived, after=()):
        for s in order:
            waits = list(after) + (log[-FLIGHT:][:1] if len(log) >= FLIGHT else [])
            message = messages[s]
            if waits:
                (message,) = gated(f"gate_{name}_{s}", [message], waits)
            arrived[s] = lax.ppermute(message, axes, [(i, i ^ s) for i in range(parts)])
            log.append(arrived[s])

    def mixed(some_far, some_near):
        out = []
        while some_far or some_near:
            out += some_far[:2] + some_near[:1] if some_far else some_near
            some_near = some_near[1:] if some_far else []
            some_far = some_far[2:]
        return out

    made = front(
        1,
        parts,
        me,
        voltages,
        coeffs,
        tables,
        [(width * 2 * TBLK, BLK)] * parts,
        lambda s, parity, channel: (s, parity * half + channel),
    )
    late, earlier = {0: made[0]}, made[parts + 1]
    history = passed_along(made[parts], "freq", 1)
    log.append(history)
    ahead = FLIGHT - 1
    send("late", made, far[:ahead], late)

    made_early = front(
        0,
        parts,
        me,
        voltages,
        coeffs,
        tables,
        [((half + extra) * 2 * TBLK + TBLK, BLK)] * parts + [((half - extra) * 2 * TBLK, BLK)] * parts,
        lambda s, parity, channel: (
            (s, parity * half + channel)
            if parity == 0 or channel < extra
            else (parts + s, channel - extra)
        ),
        history,
        earlier,
    )
    send("late", made, mixed(far[ahead:], near), late, [made_early[-1]])
    one, two = made_early[:parts], made_early[parts : 2 * parts]
    early, rest = {0: one[0]}, {0: two[0]}
    send("one", one, mixed(far, near), early)

    def every(found):
        return [found[s] for s in range(parts)]

    send("two", two, far[:FLIGHT], rest)
    late, early = every(late), every(early)
    left_far, left_near = far[FLIGHT:], list(near)
    out, after = None, []
    pieces = [(parity, i) for parity, size in ((0, half), (1, extra)) for i in range(0, size, extra)]
    for parity, i in pieces:
        spot = (parity * half + i, parity * half + i)
        out, token = correlated(
            f"correlate_{parity}_{i}", me, late, early, early, spot, extra, 2 * i + parity, width, out, after
        )
        final = (parity, i) == pieces[-1]
        now = left_near if final else left_near[:1]
        send("two", two, now + left_far[: len(left_far) if final else 1], rest, [token])
        after = [rest[now[0]]] if now else []
        left_near, left_far = left_near[1:], left_far[1:]
    out, _ = correlated(
        "correlate_rest",
        me,
        late,
        every(rest),
        early,
        (half + extra, 0),
        half - extra,
        2 * extra + 1,
        width,
        out,
    )
    return out


def solution(mesh):
    in_specs = (P(("grp", "inp"), "freq", None), P())
    out_specs = P(("grp", "inp", "freq"), None, None, None, None)
    return jax.shard_map(
        per_device, mesh=mesh, in_specs=in_specs, out_specs=out_specs, check_vma=False
    )
```

```python
import math

import jax
import jax.numpy as jnp
import ml_dtypes
import numpy as np
from jax import lax
from jax.experimental import pallas as pl
from jax.experimental.pallas import tpu as pltpu
from jax.sharding import PartitionSpec as P

SPF = 2048
TAPS = 8
CH = 512
CH0 = 256
INPUTS = 1024
BLK = 128
LANES = 128
UBLK = 16
TBLK = 16
VMEM_BYTES = 64 * 2**20 - 2**16
FLIGHT = 5
PITCH = TBLK + 1


def passed_along(x, axis, by):
    length = lax.axis_size(axis)
    pairs = [(i, i + by) for i in range(length) if 0 <= i + by < length]
    return lax.ppermute(x, axis, pairs)


def make_table():
    sample = jnp.arange(SPF, dtype=jnp.int32)[:, None]
    channel = jnp.arange(CH, dtype=jnp.int32)[None, :] + CH0
    phase = sample * channel % SPF
    angle = phase.astype(jnp.float32) * (2.0 * math.pi / SPF)
    return jnp.concatenate([jnp.cos(angle), -jnp.sin(angle)], axis=1).astype(jnp.bfloat16)


def any_sizes(voltages, coeffs):
    inputs_here = voltages.shape[0]
    frames_here = voltages.shape[1]
    inp_count = lax.axis_size("inp")
    freq_count = lax.axis_size("freq")
    frames_all = frames_here * freq_count
    history = voltages[:, frames_here - (TAPS - 1) :, :].astype(jnp.bfloat16)
    earlier = passed_along(history, "freq", 1)
    extended = jnp.concatenate([earlier.astype(jnp.float32), voltages.astype(jnp.float32)], axis=1)
    weights = coeffs.astype(jnp.float32)
    summed = jnp.zeros((inputs_here, frames_here, SPF), jnp.float32)
    for tap_index in range(TAPS):
        begin = TAPS - 1 - tap_index
        summed = summed + weights[tap_index] * extended[:, begin : begin + frames_here, :]
    filtered = summed.astype(jnp.bfloat16).reshape(inputs_here * frames_here, SPF)
    spectrum_t = jnp.einsum("nj,rn->jr", make_table(), filtered, preferred_element_type=jnp.float32)
    spectrum_t = spectrum_t.reshape(2 * CH, inputs_here, frames_here)
    squares = jnp.sum(spectrum_t * spectrum_t, axis=(0, 2))
    power = lax.psum(squares, "freq") / (frames_all * CH)
    gains = 1.0 / jnp.sqrt(power + 1e-06)
    scaled = (spectrum_t * gains[None, :, None]).astype(jnp.bfloat16)
    scaled = scaled.reshape(2, CH, inputs_here * frames_here)
    arrived = lax.all_to_all(scaled[None], ("inp", "freq"), split_axis=2, concat_axis=0, tiled=True)
    width_here = arrived.shape[-2]
    arranged = arrived.reshape(inp_count, freq_count, 2, width_here, inputs_here, frames_here)
    arranged = jnp.transpose(arranged, (3, 0, 4, 2, 1, 5))
    stacked = arranged.reshape(width_here, INPUTS, 2 * frames_all)
    other = jnp.concatenate([-stacked[:, :, frames_all:], stacked[:, :, :frames_all]], axis=2)
    block_count = INPUTS // BLK
    scale = 1.0 / frames_all
    pieces = []
    for row_index in range(block_count):
        row_panel = stacked[:, row_index * BLK : (row_index + 1) * BLK]
        real_part = jnp.einsum(
            "cut,cmt->cum",
            row_panel,
            stacked[:, row_index * BLK :],
            preferred_element_type=jnp.float32,
        )
        imag_part = jnp.einsum(
            "cut,cmt->cum",
            row_panel,
            other[:, row_index * BLK :],
            preferred_element_type=jnp.float32,
        )
        band = jnp.stack([real_part, imag_part], axis=1) * scale
        for col_index in range(row_index, block_count):
            begin = (col_index - row_index) * BLK
            pieces.append(band[:, :, :, begin : begin + BLK])
    return jnp.stack(pieces, axis=2).astype(jnp.bfloat16)


def turned_over(rows):
    rows = list(rows)
    place = lax.broadcasted_iota(jnp.int32, (8, LANES), 0)
    for shift in (4, 2, 1):
        low = jnp.bitwise_and(place, shift) == 0
        for i in range(8):
            if i & shift == 0:
                near, far = rows[i], rows[i + shift]
                rows[i] = jnp.where(low, near, pltpu.roll(far, shift, 0))
                rows[i + shift] = jnp.where(low, pltpu.roll(near, 8 - shift, 0), far)
    return rows


def frames_of(v_ref, cols):
    groups = []
    for group in range(UBLK // 8):
        groups.append(turned_over([v_ref[group * 8 + i, :, cols] for i in range(8)]))
    return [[group[t].astype(jnp.float32) for group in groups] for t in range(8)]


def kept(array):
    return pltpu.with_memory_space_constraint(array, pltpu.HBM)


def parity_tables(parts, width):
    tables = []
    for parity in range(2):
        within = np.arange(parity, width, 2)
        channel = (np.arange(parts)[:, None] * width + within[None, :]).reshape(-1) + CH0
        phase = channel[:, None].astype(np.int64) * np.arange(SPF // 2)[None, :] % SPF
        angle = phase.astype(np.float32) * np.float32(2.0 * math.pi / SPF)
        wide = angle.astype(np.float64)
        both = np.stack([np.cos(wide), -np.sin(wide)], axis=1)
        both = both.reshape(-1, SPF // 2).astype(np.float32)
        tables.append(jnp.asarray(both.astype(ml_dtypes.bfloat16)))
    return tables


def filter_step(block, sources, c_ref, even, odd, last_ref):
    half = SPF // 2
    groups = UBLK // 8
    here = pl.ds(pl.multiple_of(pl.program_id(0) * UBLK, UBLK), UBLK)

    def column(step, carry):
        sides = []
        before = []
        for side in range(2):
            cols = pl.ds(pl.multiple_of(step * LANES + side * half, LANES), LANES)
            weights = c_ref[:, cols].astype(jnp.float32)
            taps = [jnp.broadcast_to(weights[k : k + 1], (8, LANES)) for k in range(TAPS)]
            sides.append((cols, taps))
            if block == 0:
                wide = [sources[0][t, :, cols].astype(jnp.float32) for t in range(TAPS)]
                before.append([[w[g * 8 : (g + 1) * 8] for g in range(groups)] for w in wide])
            else:
                before.append(frames_of(sources[0], cols))
        out = pl.ds(pl.multiple_of(step * LANES, LANES), LANES)
        for part in range(TBLK // TAPS):
            made = []
            for side, (cols, taps) in enumerate(sides):
                now = frames_of(sources[1 + part], cols)
                window = before[side] + now
                before[side] = now
                totals = []
                for t in range(TAPS):
                    frame = []
                    for g in range(groups):
                        total = taps[0] * window[TAPS + t][g]
                        for k in range(1, TAPS):
                            total = total + taps[k] * window[TAPS + t - k][g]
                        frame.append(total)
                    totals.append(jnp.concatenate(frame, axis=0))
                made.append(totals)
                if last_ref is not None and part == TBLK // TAPS - 1:
                    for t in range(TAPS):
                        frame = jnp.concatenate(now[t], axis=0)
                        last_ref[t, :, cols] = frame.astype(jnp.bfloat16)
            for t in range(TAPS):
                at = part * TAPS + t
                even[at, here, out] = (made[0][t] + made[1][t]).astype(jnp.bfloat16)
                odd[at, here, out] = (made[0][t] - made[1][t]).astype(jnp.bfloat16)
        return carry

    lax.fori_loop(0, half // LANES, column, 0)


def front_kernel(block, parts, where, me_ref, *refs):
    count = 1 + TBLK // TAPS
    sources, c_ref, tables = refs[:count], refs[count], refs[count + 1 : count + 3]
    earlier_ref = refs[count + 3] if block == 0 else None
    outs = refs[count + (4 if block == 0 else 3) : -4]
    last_ref = None if block == 0 else outs[-1]
    power_ref, even, odd, turned = refs[-4:]
    filter_step(block, sources, c_ref, even, odd, last_ref)

    @pl.when(pl.program_id(0) == pl.num_programs(0) - 1)
    def _():
        me = me_ref[0]
        square = jnp.zeros((8, BLK), jnp.float32)
        for parity, filtered in enumerate((even, odd)):
            rows = tables[parity].shape[0]
            own = rows // parts
            spectrum = lax.dot_general(
                tables[parity][...],
                filtered[...].reshape(-1, SPF // 2),
                (((1,), (1,)), ((), ())),
                preferred_element_type=jnp.float32,
            )
            for t in range(TBLK):
                frame = spectrum[:, t * BLK : (t + 1) * BLK]
                turned[pl.ds(t, rows, stride=PITCH), :] = frame
                square = square + jnp.sum((frame * frame).reshape(rows // 8, 8, BLK), axis=0)
            for s in range(parts):
                begin = jnp.bitwise_xor(me, s) * (own * PITCH)
                for channel in range(own // 2):
                    index, place = where(s, parity, channel)
                    for half in range(2):
                        row = channel * 2 + half
                        value = turned[pl.ds(begin + row * PITCH, TBLK), :].astype(jnp.bfloat16)
                        to = (place * 2 + half) * TBLK
                        outs[index][to : to + TBLK, :] = value
        if block == 0:
            square = square + earlier_ref[...]
            rest = jnp.sum(square, axis=0, keepdims=True)
            terms = []
            for _ in range(3):
                term = rest.astype(jnp.bfloat16).astype(jnp.float32)
                terms.append(term)
                rest = rest - term
            terms.append(jnp.zeros((TBLK - 3, BLK), jnp.float32))
            tail = jnp.concatenate(terms, axis=0).astype(jnp.bfloat16)
            for s in range(parts):
                size = outs[s].shape[0]
                outs[s][size - TBLK :, :] = tail
        power_ref[...] = square


def front(block, parts, me, voltages, coeffs, tables, shapes, where, history=None, earlier=None):
    inputs, frames, _ = voltages.shape
    half = SPF // 2
    first = block * (TBLK // TAPS)
    in_specs, operands = [], []
    for place in range(first - 1, first + TBLK // TAPS):
        if place < 0:
            in_specs.append(pl.BlockSpec((TAPS, UBLK, SPF), lambda i, me: (0, i, 0)))
            operands.append(kept(history))
        else:
            in_specs.append(
                pl.BlockSpec((UBLK, TAPS, SPF), lambda i, me, place=place: (i, place, 0))
            )
            operands.append(voltages)
    operands += [coeffs, *tables]
    if block == 0:
        operands.append(earlier)
    for array in operands[len(in_specs) :]:
        in_specs.append(pl.BlockSpec(array.shape, lambda i, me: (0, 0)))
    out_shapes = [pltpu.HBM(shape, jnp.bfloat16) for shape in shapes]
    out_specs = [pl.BlockSpec(shape, lambda i, me: (0, 0)) for shape in shapes]
    if block == 1:
        out_shapes.append(pltpu.HBM((TAPS, inputs, SPF), jnp.bfloat16))
        out_specs.append(pl.BlockSpec((TAPS, UBLK, SPF), lambda i, me: (0, i, 0)))
    out_shapes.append(jax.ShapeDtypeStruct((8, BLK), jnp.float32))
    out_specs.append(pl.BlockSpec((8, BLK), lambda i, me: (0, 0)))

    def kernel(me_ref, *refs):
        front_kernel(block, parts, where, me_ref, *refs)

    return pl.pallas_call(
        kernel,
        name=f"front_{block}",
        grid_spec=pltpu.PrefetchScalarGridSpec(
            num_scalar_prefetch=1,
            grid=(inputs // UBLK,),
            in_specs=in_specs,
            out_specs=out_specs,
            scratch_shapes=[
                pltpu.VMEM((TBLK, inputs, half), jnp.bfloat16),
                pltpu.VMEM((TBLK, inputs, half), jnp.bfloat16),
                pltpu.VMEM((tables[0].shape[0] * PITCH + 8, BLK), jnp.float32),
            ],
        ),
        out_shape=out_shapes,
        compiler_params=pltpu.CompilerParams(vmem_limit_bytes=VMEM_BYTES),
    )(me, *operands)


def correlate_kernel(parts, me_ref, *refs):
    late, early, powers = refs[:parts], refs[parts : 2 * parts], refs[2 * parts : 3 * parts]
    out_ref, token_ref, plain, other, columns, lines, shares = refs[-7:]
    blocks = INPUTS // BLK
    freq = parts // blocks
    me = me_ref[0]

    @pl.when(pl.program_id(0) == 0)
    def _():
        token_ref[...] = jnp.zeros_like(token_ref)
        for s in range(parts):
            terms = powers[s][...].astype(jnp.float32)
            power = terms[0:1] + terms[1:2] + terms[2:3]
            shares[jnp.bitwise_xor(me, s)] = jnp.broadcast_to(power, (8, BLK))
        for r in range(blocks):
            power = shares[r * freq]
            for f in range(1, freq):
                power = power + shares[r * freq + f]
            gain = 1.0 / jnp.sqrt(power / (freq * 2 * TBLK * CH) + 1e-06)
            lines[r] = gain
            columns[r * BLK : (r + 1) * BLK, :] = jnp.broadcast_to(gain[0:1], (BLK, BLK)).T

    for s in range(parts):
        source = jnp.bitwise_xor(me, s)
        block, place = source // freq, source % freq
        for half, ref in enumerate((late[s], early[s])):
            begin = pl.multiple_of((place * 2 + half) * 2 * TBLK, 2 * TBLK)
            real = ref[:TBLK, :]
            imag = ref[TBLK:, :]
            plain[block, pl.ds(begin, TBLK), :] = real
            plain[block, pl.ds(begin + TBLK, TBLK), :] = imag
            other[block, pl.ds(begin, TBLK), :] = -imag
            other[block, pl.ds(begin + TBLK, TBLK), :] = real

    sides = [plain[r].T for r in range(blocks)]
    for c in range(blocks):
        weights = jnp.concatenate([plain[c], other[c]], axis=1)
        line = lines[c][0:1] * (1.0 / (freq * 2 * TBLK))
        for r in range(c + 1):
            both = jnp.dot(sides[r], weights, preferred_element_type=jnp.float32)
            pair = r * blocks - r * (r - 1) // 2 + (c - r)
            gain = columns[r * BLK : (r + 1) * BLK, :] * line
            for part in range(2):
                piece = both[:, part * BLK : (part + 1) * BLK]
                out_ref[0, part, pair] = (piece * gain).astype(jnp.bfloat16)


def correlated(name, me, late, early, powers, spot, count, width, before, after=()):
    parts = len(late)
    blocks = INPUTS // BLK
    pairs = blocks * (blocks + 1) // 2
    span = parts // blocks * 4 * TBLK
    first, second = spot
    last = powers[0].shape[0] // TBLK - 1
    in_specs = (
        [pl.BlockSpec((2 * TBLK, BLK), lambda i, me: (first + i, 0))] * parts
        + [pl.BlockSpec((2 * TBLK, BLK), lambda i, me: (second + i, 0))] * parts
        + [pl.BlockSpec((TBLK, BLK), lambda i, me: (last, 0))] * parts
    )
    operands = [me, *map(kept, late), *map(kept, early), *map(kept, powers)]
    aliases = {}
    if before is not None:
        aliases[len(operands)] = 0
        operands.append(before)
    operands += map(kept, after)
    in_specs += [pl.BlockSpec(memory_space=pl.ANY)] * (len(operands) - 1 - len(in_specs))

    def kernel(me_ref, *refs):
        correlate_kernel(parts, me_ref, *refs)

    return pl.pallas_call(
        kernel,
        name=name,
        grid_spec=pltpu.PrefetchScalarGridSpec(
            num_scalar_prefetch=1,
            grid=(count,),
            in_specs=in_specs,
            out_specs=[
                pl.BlockSpec(
                    (1, 2, pairs, BLK, BLK),
                    lambda i, me: (
                        2 * lax.rem(first + i, width // 2) + lax.div(first + i, width // 2),
                        0,
                        0,
                        0,
                        0,
                    ),
                ),
                pl.BlockSpec((8, BLK), lambda i, me: (0, 0)),
            ],
            scratch_shapes=[
                pltpu.VMEM((blocks, span, BLK), jnp.bfloat16),
                pltpu.VMEM((blocks, span, BLK), jnp.bfloat16),
                pltpu.VMEM((INPUTS, BLK), jnp.float32),
                pltpu.VMEM((blocks, 8, BLK), jnp.float32),
                pltpu.VMEM((parts, 8, BLK), jnp.float32),
            ],
        ),
        out_shape=[
            jax.ShapeDtypeStruct((width, 2, pairs, BLK, BLK), jnp.bfloat16),
            jax.ShapeDtypeStruct((8, BLK), jnp.float32),
        ],
        input_output_aliases=aliases,
        compiler_params=pltpu.CompilerParams(vmem_limit_bytes=VMEM_BYTES),
    )(*operands)


def nothing_kernel(*refs):
    del refs


def gated(name, messages, after):
    spec = pl.BlockSpec(memory_space=pl.ANY)
    return pl.pallas_call(
        nothing_kernel,
        name=name,
        in_specs=[spec] * (len(messages) + len(after)),
        out_specs=[spec] * len(messages),
        out_shape=[pltpu.HBM(m.shape, m.dtype) for m in messages],
        input_output_aliases={i: i for i in range(len(messages))},
        compiler_params=pltpu.CompilerParams(vmem_limit_bytes=VMEM_BYTES),
    )(*map(kept, messages), *map(kept, after))


def per_device(voltages, coeffs):
    freq_count = lax.axis_size("freq")
    parts = lax.axis_size("inp") * freq_count
    inputs, frames, _ = voltages.shape
    width = CH // parts
    fits = (
        inputs == BLK
        and frames == 2 * TBLK
        and TBLK % TAPS == 0
        and parts & (parts - 1) == 0
        and parts >= 16
        and width % 16 == 0
        and parts * BLK == INPUTS * freq_count
        and freq_count * frames * 2 == LANES
    )
    if not fits:
        return any_sizes(voltages, coeffs)
    axes = ("inp", "freq")
    me = lax.axis_index("inp") * freq_count + lax.axis_index("freq")
    me = me.astype(jnp.int32).reshape(1)
    half = width // 2
    tables = parity_tables(parts, width)
    sizes = [width * 7 // 16, width * 5 // 16, width // 4]
    starts = [0, sizes[0], sizes[0] + sizes[1]]

    far, near = list(range(parts // 2, parts)), list(range(1, parts // 2))
    far = [s for pair in zip(far[: parts // 4], far[parts // 4 :]) for s in pair]
    near = near[parts // 4 - 1 :] + near[: parts // 4 - 1]
    log, passed = [], []

    def send(chunk, s, after=()):
        waits = list(after) + (log[-FLIGHT:][:1] if len(log) >= FLIGHT else [])
        message = messages[chunk][s]
        if waits:
            (message,) = gated(f"gate_{chunk}_{s}", [message], waits + passed)
            passed[:] = [message]
        arrived[chunk][s] = lax.ppermute(message, axes, [(i, i ^ s) for i in range(parts)])
        log.append(arrived[chunk][s])

    made = front(
        1,
        parts,
        me,
        voltages,
        coeffs,
        tables,
        [(width * 2 * TBLK, BLK)] * parts,
        lambda s, parity, channel: (s, parity * half + channel),
    )
    messages, arrived = [made[:parts]], [{0: made[0]}]
    history, earlier = made[parts], made[parts + 1]
    history = passed_along(history, "freq", 1)
    log.append(history)
    for s in far[: FLIGHT - 1]:
        send(0, s)

    def where(s, parity, channel):
        place = parity * half + channel
        chunk = max(i for i in range(len(starts)) if starts[i] <= place)
        return chunk * parts + s, place - starts[chunk]

    shapes = [(size * 2 * TBLK + (TBLK if i == 0 else 0), BLK) for i, size in enumerate(sizes)]
    made = front(
        0,
        parts,
        me,
        voltages,
        coeffs,
        tables,
        [shape for shape in shapes for _ in range(parts)],
        where,
        history,
        earlier,
    )
    for i in range(len(sizes)):
        messages.append(made[i * parts : (i + 1) * parts])
        arrived.append({0: made[i * parts]})
    done = [made[-1]]

    far_left = [(0, s) for s in far[FLIGHT - 1 :]] + [(1, s) for s in far]
    near_left = [(0, s) for s in near] + [(1, s) for s in near]
    lead = len(near_left) - len(far_left)
    while far_left or near_left:
        take = [near_left.pop(0)] if near_left else []
        if lead > 0 and near_left and len(far_left) % 4 == 0:
            take.append(near_left.pop(0))
            lead -= 1
        if far_left:
            take.append(far_left.pop(0))
        for chunk, s in take:
            send(chunk, s, done)

    def every(chunk):
        return [arrived[chunk][s] for s in range(parts)]

    out, token = None, done[0]
    for chunk in range(1, len(sizes) + 1):
        size, start = sizes[chunk - 1], starts[chunk - 1]
        if chunk == len(sizes):
            pieces = [size]
        else:
            pieces = [size - size // 2, size // 2]
            far_left, near_left = list(far), near[parts // 4 :] + near[: parts // 4]
            for s in far_left[: FLIGHT - 1]:
                send(chunk + 1, s, [token])
            far_left = far_left[FLIGHT - 1 :]
        after = []
        for index, count in enumerate(pieces):
            first = sum(pieces[:index])
            out, token = correlated(
                f"correlate_{chunk}_{index}",
                me,
                every(0),
                every(chunk),
                every(1),
                (start + first, first),
                count,
                width,
                out,
                after,
            )
            if chunk == len(sizes):
                break
            final = index == len(pieces) - 1
            first_near = near_left[0]
            for turn in range(len(near_left) if final else 3):
                if near_left:
                    send(chunk + 1, near_left.pop(0), [token])
                if far_left and turn < (len(near) if final else 2):
                    send(chunk + 1, far_left.pop(0), [token])
            after = [arrived[chunk + 1][first_near]]
    return out


def solution(mesh):
    in_specs = (P(("grp", "inp"), "freq", None), P())
    out_specs = P(("grp", "inp", "freq"), None, None, None, None)
    return jax.shard_map(
        per_device, mesh=mesh, in_specs=in_specs, out_specs=out_specs, check_vma=False
    )
```

```python
import math

import jax
import jax.numpy as jnp
import ml_dtypes
import numpy as np
from jax import lax
from jax.experimental import pallas as pl
from jax.experimental.pallas import tpu as pltpu
from jax.sharding import PartitionSpec as P

SPF = 2048
TAPS = 8
CH = 512
CH0 = 256
INPUTS = 1024
BLK = 128
LANES = 128
UBLK = 16
TBLK = 16
VMEM_BYTES = 64 * 2**20 - 2**16
FLIGHT = 5
PITCH = TBLK + 1


def passed_along(x, axis, by):
    length = lax.axis_size(axis)
    pairs = [(i, i + by) for i in range(length) if 0 <= i + by < length]
    return lax.ppermute(x, axis, pairs)


def make_table():
    sample = jnp.arange(SPF, dtype=jnp.int32)[:, None]
    channel = jnp.arange(CH, dtype=jnp.int32)[None, :] + CH0
    phase = sample * channel % SPF
    angle = phase.astype(jnp.float32) * (2.0 * math.pi / SPF)
    return jnp.concatenate([jnp.cos(angle), -jnp.sin(angle)], axis=1).astype(jnp.bfloat16)


def any_sizes(voltages, coeffs):
    inputs_here = voltages.shape[0]
    frames_here = voltages.shape[1]
    inp_count = lax.axis_size("inp")
    freq_count = lax.axis_size("freq")
    frames_all = frames_here * freq_count
    history = voltages[:, frames_here - (TAPS - 1) :, :].astype(jnp.bfloat16)
    earlier = passed_along(history, "freq", 1)
    extended = jnp.concatenate([earlier.astype(jnp.float32), voltages.astype(jnp.float32)], axis=1)
    weights = coeffs.astype(jnp.float32)
    summed = jnp.zeros((inputs_here, frames_here, SPF), jnp.float32)
    for tap_index in range(TAPS):
        begin = TAPS - 1 - tap_index
        summed = summed + weights[tap_index] * extended[:, begin : begin + frames_here, :]
    filtered = summed.astype(jnp.bfloat16).reshape(inputs_here * frames_here, SPF)
    spectrum_t = jnp.einsum("nj,rn->jr", make_table(), filtered, preferred_element_type=jnp.float32)
    spectrum_t = spectrum_t.reshape(2 * CH, inputs_here, frames_here)
    squares = jnp.sum(spectrum_t * spectrum_t, axis=(0, 2))
    power = lax.psum(squares, "freq") / (frames_all * CH)
    gains = 1.0 / jnp.sqrt(power + 1e-06)
    scaled = (spectrum_t * gains[None, :, None]).astype(jnp.bfloat16)
    scaled = scaled.reshape(2, CH, inputs_here * frames_here)
    arrived = lax.all_to_all(scaled[None], ("inp", "freq"), split_axis=2, concat_axis=0, tiled=True)
    width_here = arrived.shape[-2]
    arranged = arrived.reshape(inp_count, freq_count, 2, width_here, inputs_here, frames_here)
    arranged = jnp.transpose(arranged, (3, 0, 4, 2, 1, 5))
    stacked = arranged.reshape(width_here, INPUTS, 2 * frames_all)
    other = jnp.concatenate([-stacked[:, :, frames_all:], stacked[:, :, :frames_all]], axis=2)
    block_count = INPUTS // BLK
    scale = 1.0 / frames_all
    pieces = []
    for row_index in range(block_count):
        row_panel = stacked[:, row_index * BLK : (row_index + 1) * BLK]
        real_part = jnp.einsum(
            "cut,cmt->cum",
            row_panel,
            stacked[:, row_index * BLK :],
            preferred_element_type=jnp.float32,
        )
        imag_part = jnp.einsum(
            "cut,cmt->cum",
            row_panel,
            other[:, row_index * BLK :],
            preferred_element_type=jnp.float32,
        )
        band = jnp.stack([real_part, imag_part], axis=1) * scale
        for col_index in range(row_index, block_count):
            begin = (col_index - row_index) * BLK
            pieces.append(band[:, :, :, begin : begin + BLK])
    return jnp.stack(pieces, axis=2).astype(jnp.bfloat16)


def turned_over(rows):
    rows = list(rows)
    place = lax.broadcasted_iota(jnp.int32, (8, LANES), 0)
    for shift in (4, 2, 1):
        low = jnp.bitwise_and(place, shift) == 0
        for i in range(8):
            if i & shift == 0:
                near, far = rows[i], rows[i + shift]
                rows[i] = jnp.where(low, near, pltpu.roll(far, shift, 0))
                rows[i + shift] = jnp.where(low, pltpu.roll(near, 8 - shift, 0), far)
    return rows


def frames_of(v_ref, cols):
    groups = []
    for group in range(UBLK // 8):
        groups.append(turned_over([v_ref[group * 8 + i, :, cols] for i in range(8)]))
    return [[group[t].astype(jnp.float32) for group in groups] for t in range(8)]


def kept(array):
    return pltpu.with_memory_space_constraint(array, pltpu.HBM)


def parity_tables(parts, width):
    tables = []
    for parity in range(2):
        within = np.arange(parity, width, 2)
        channel = (np.arange(parts)[:, None] * width + within[None, :]).reshape(-1) + CH0
        phase = channel[:, None].astype(np.int64) * np.arange(SPF // 2)[None, :] % SPF
        angle = phase.astype(np.float32) * np.float32(2.0 * math.pi / SPF)
        wide = angle.astype(np.float64)
        both = np.stack([np.cos(wide), -np.sin(wide)], axis=1)
        both = both.reshape(-1, SPF // 2).astype(np.float32)
        tables.append(jnp.asarray(both.astype(ml_dtypes.bfloat16)))
    return tables


def filter_step(block, sources, c_ref, even, odd, last_ref):
    half = SPF // 2
    groups = UBLK // 8
    here = pl.ds(pl.multiple_of(pl.program_id(0) * UBLK, UBLK), UBLK)

    def column(step, carry):
        sides = []
        before = []
        for side in range(2):
            cols = pl.ds(pl.multiple_of(step * LANES + side * half, LANES), LANES)
            weights = c_ref[:, cols].astype(jnp.float32)
            taps = [jnp.broadcast_to(weights[k : k + 1], (8, LANES)) for k in range(TAPS)]
            sides.append((cols, taps))
            if block == 0:
                wide = [sources[0][t, :, cols].astype(jnp.float32) for t in range(TAPS)]
                before.append([[w[g * 8 : (g + 1) * 8] for g in range(groups)] for w in wide])
            else:
                before.append(frames_of(sources[0], cols))
        out = pl.ds(pl.multiple_of(step * LANES, LANES), LANES)
        for part in range(TBLK // TAPS):
            made = []
            for side, (cols, taps) in enumerate(sides):
                now = frames_of(sources[1 + part], cols)
                window = before[side] + now
                before[side] = now
                totals = []
                for t in range(TAPS):
                    frame = []
                    for g in range(groups):
                        total = taps[0] * window[TAPS + t][g]
                        for k in range(1, TAPS):
                            total = total + taps[k] * window[TAPS + t - k][g]
                        frame.append(total)
                    totals.append(jnp.concatenate(frame, axis=0))
                made.append(totals)
                if last_ref is not None and part == TBLK // TAPS - 1:
                    for t in range(TAPS):
                        frame = jnp.concatenate(now[t], axis=0)
                        last_ref[t, :, cols] = frame.astype(jnp.bfloat16)
            for t in range(TAPS):
                at = part * TAPS + t
                even[at, here, out] = (made[0][t] + made[1][t]).astype(jnp.bfloat16)
                odd[at, here, out] = (made[0][t] - made[1][t]).astype(jnp.bfloat16)
        return carry

    lax.fori_loop(0, half // LANES, column, 0)


def front_kernel(block, parts, where, me_ref, *refs):
    count = 1 + TBLK // TAPS
    sources, c_ref, tables = refs[:count], refs[count], refs[count + 1 : count + 3]
    earlier_ref = refs[count + 3] if block == 0 else None
    outs = refs[count + (4 if block == 0 else 3) : -4]
    last_ref = None if block == 0 else outs[-1]
    power_ref, even, odd, turned = refs[-4:]
    filter_step(block, sources, c_ref, even, odd, last_ref)

    @pl.when(pl.program_id(0) == pl.num_programs(0) - 1)
    def _():
        me = me_ref[0]
        square = jnp.zeros((8, BLK), jnp.float32)
        for parity, filtered in enumerate((even, odd)):
            rows = tables[parity].shape[0]
            own = rows // parts
            spectrum = lax.dot_general(
                tables[parity][...],
                filtered[...].reshape(-1, SPF // 2),
                (((1,), (1,)), ((), ())),
                preferred_element_type=jnp.float32,
            )
            for t in range(TBLK):
                frame = spectrum[:, t * BLK : (t + 1) * BLK]
                turned[pl.ds(t, rows, stride=PITCH), :] = frame
                square = square + jnp.sum((frame * frame).reshape(rows // 8, 8, BLK), axis=0)
            for s in range(parts):
                begin = jnp.bitwise_xor(me, s) * (own * PITCH)
                for channel in range(own // 2):
                    index, place = where(s, parity, channel)
                    for half in range(2):
                        row = channel * 2 + half
                        value = turned[pl.ds(begin + row * PITCH, TBLK), :].astype(jnp.bfloat16)
                        to = (place * 2 + half) * TBLK
                        outs[index][to : to + TBLK, :] = value
        if block == 0:
            square = square + earlier_ref[...]
            rest = jnp.sum(square, axis=0, keepdims=True)
            terms = []
            for _ in range(3):
                term = rest.astype(jnp.bfloat16).astype(jnp.float32)
                terms.append(term)
                rest = rest - term
            terms.append(jnp.zeros((TBLK - 3, BLK), jnp.float32))
            tail = jnp.concatenate(terms, axis=0).astype(jnp.bfloat16)
            for s in range(parts):
                size = outs[s].shape[0]
                outs[s][size - TBLK :, :] = tail
        power_ref[...] = square


def front(block, parts, me, voltages, coeffs, tables, shapes, where, history=None, earlier=None):
    inputs, frames, _ = voltages.shape
    half = SPF // 2
    first = block * (TBLK // TAPS)
    in_specs, operands = [], []
    for place in range(first - 1, first + TBLK // TAPS):
        if place < 0:
            in_specs.append(pl.BlockSpec((TAPS, UBLK, SPF), lambda i, me: (0, i, 0)))
            operands.append(kept(history))
        else:
            in_specs.append(
                pl.BlockSpec((UBLK, TAPS, SPF), lambda i, me, place=place: (i, place, 0))
            )
            operands.append(voltages)
    operands += [coeffs, *tables]
    if block == 0:
        operands.append(earlier)
    for array in operands[len(in_specs) :]:
        in_specs.append(pl.BlockSpec(array.shape, lambda i, me: (0, 0)))
    out_shapes = [pltpu.HBM(shape, jnp.bfloat16) for shape in shapes]
    out_specs = [pl.BlockSpec(shape, lambda i, me: (0, 0)) for shape in shapes]
    if block == 1:
        out_shapes.append(pltpu.HBM((TAPS, inputs, SPF), jnp.bfloat16))
        out_specs.append(pl.BlockSpec((TAPS, UBLK, SPF), lambda i, me: (0, i, 0)))
    out_shapes.append(jax.ShapeDtypeStruct((8, BLK), jnp.float32))
    out_specs.append(pl.BlockSpec((8, BLK), lambda i, me: (0, 0)))

    def kernel(me_ref, *refs):
        front_kernel(block, parts, where, me_ref, *refs)

    return pl.pallas_call(
        kernel,
        name=f"front_{block}",
        grid_spec=pltpu.PrefetchScalarGridSpec(
            num_scalar_prefetch=1,
            grid=(inputs // UBLK,),
            in_specs=in_specs,
            out_specs=out_specs,
            scratch_shapes=[
                pltpu.VMEM((TBLK, inputs, half), jnp.bfloat16),
                pltpu.VMEM((TBLK, inputs, half), jnp.bfloat16),
                pltpu.VMEM((tables[0].shape[0] * PITCH + 8, BLK), jnp.float32),
            ],
        ),
        out_shape=out_shapes,
        compiler_params=pltpu.CompilerParams(vmem_limit_bytes=VMEM_BYTES),
    )(me, *operands)


def correlate_kernel(parts, first, count, me_ref, *refs):
    late, early, powers = refs[:parts], refs[parts : 2 * parts], refs[2 * parts : 3 * parts]
    out_ref, token_ref, plain, other, columns, lines, shares, ready, sems = refs[-9:]
    blocks = INPUTS // BLK
    freq = parts // blocks
    me = me_ref[0]

    step = pl.program_id(0)
    slot = lax.rem(step, 2)
    depth = out_ref.shape[0]

    def writes(step, slot):
        channel = 2 * lax.rem(first + step, depth // 2) + lax.div(first + step, depth // 2)
        return [
            pltpu.make_async_copy(
                ready.at[slot, part], out_ref.at[channel, part], sems.at[slot, part]
            )
            for part in range(2)
        ]

    @pl.when(step >= 2)
    def _():
        for write in writes(step - 2, slot):
            write.wait()

    @pl.when(step == 0)
    def _():
        token_ref[...] = jnp.zeros_like(token_ref)
        for s in range(parts):
            terms = powers[s][...].astype(jnp.float32)
            power = terms[0:1] + terms[1:2] + terms[2:3]
            shares[jnp.bitwise_xor(me, s)] = jnp.broadcast_to(power, (8, BLK))
        for r in range(blocks):
            power = shares[r * freq]
            for f in range(1, freq):
                power = power + shares[r * freq + f]
            gain = 1.0 / jnp.sqrt(power / (freq * 2 * TBLK * CH) + 1e-06)
            lines[r] = gain
            columns[r * BLK : (r + 1) * BLK, :] = jnp.broadcast_to(gain[0:1], (BLK, BLK)).T

    for s in range(parts):
        source = jnp.bitwise_xor(me, s)
        block, place = source // freq, source % freq
        for half, ref in enumerate((late[s], early[s])):
            begin = pl.multiple_of((place * 2 + half) * 2 * TBLK, 2 * TBLK)
            real = ref[:TBLK, :]
            imag = ref[TBLK:, :]
            plain[block, pl.ds(begin, TBLK), :] = real
            plain[block, pl.ds(begin + TBLK, TBLK), :] = imag
            other[block, pl.ds(begin, TBLK), :] = -imag
            other[block, pl.ds(begin + TBLK, TBLK), :] = real

    sides = [plain[r].T for r in range(blocks)]
    for c in range(blocks):
        weights = jnp.concatenate([plain[c], other[c]], axis=1)
        line = lines[c][0:1] * (1.0 / (freq * 2 * TBLK))
        for r in range(c + 1):
            both = jnp.dot(sides[r], weights, preferred_element_type=jnp.float32)
            pair = r * blocks - r * (r - 1) // 2 + (c - r)
            gain = columns[r * BLK : (r + 1) * BLK, :] * line
            for part in range(2):
                piece = both[:, part * BLK : (part + 1) * BLK]
                ready[slot, part, pair] = (piece * gain).astype(jnp.bfloat16)

    for write in writes(step, slot):
        write.start()

    @pl.when(step == count - 1)
    def _():
        if count > 1:
            for write in writes(step - 1, 1 - slot):
                write.wait()
        for write in writes(step, slot):
            write.wait()


def correlated(name, me, late, early, powers, spot, count, width, before, after=()):
    parts = len(late)
    blocks = INPUTS // BLK
    pairs = blocks * (blocks + 1) // 2
    span = parts // blocks * 4 * TBLK
    first, second = spot
    last = powers[0].shape[0] // TBLK - 1
    in_specs = (
        [pl.BlockSpec((2 * TBLK, BLK), lambda i, me: (first + i, 0))] * parts
        + [pl.BlockSpec((2 * TBLK, BLK), lambda i, me: (second + i, 0))] * parts
        + [pl.BlockSpec((TBLK, BLK), lambda i, me: (last, 0))] * parts
    )
    operands = [me, *map(kept, late), *map(kept, early), *map(kept, powers)]
    aliases = {}
    if before is not None:
        aliases[len(operands)] = 0
        operands.append(before)
    operands += map(kept, after)
    in_specs += [pl.BlockSpec(memory_space=pl.ANY)] * (len(operands) - 1 - len(in_specs))

    def kernel(me_ref, *refs):
        correlate_kernel(parts, first, count, me_ref, *refs)

    return pl.pallas_call(
        kernel,
        name=name,
        grid_spec=pltpu.PrefetchScalarGridSpec(
            num_scalar_prefetch=1,
            grid=(count,),
            in_specs=in_specs,
            out_specs=[
                pl.BlockSpec(memory_space=pl.ANY),
                pl.BlockSpec((8, BLK), lambda i, me: (0, 0)),
            ],
            scratch_shapes=[
                pltpu.VMEM((blocks, span, BLK), jnp.bfloat16),
                pltpu.VMEM((blocks, span, BLK), jnp.bfloat16),
                pltpu.VMEM((INPUTS, BLK), jnp.float32),
                pltpu.VMEM((blocks, 8, BLK), jnp.float32),
                pltpu.VMEM((parts, 8, BLK), jnp.float32),
                pltpu.VMEM((2, 2, pairs, BLK, BLK), jnp.bfloat16),
                pltpu.SemaphoreType.DMA((2, 2)),
            ],
        ),
        out_shape=[
            jax.ShapeDtypeStruct((width, 2, pairs, BLK, BLK), jnp.bfloat16),
            jax.ShapeDtypeStruct((8, BLK), jnp.float32),
        ],
        input_output_aliases=aliases,
        compiler_params=pltpu.CompilerParams(vmem_limit_bytes=VMEM_BYTES),
    )(*operands)


def nothing_kernel(*refs):
    del refs


def gated(name, messages, after):
    spec = pl.BlockSpec(memory_space=pl.ANY)
    return pl.pallas_call(
        nothing_kernel,
        name=name,
        in_specs=[spec] * (len(messages) + len(after)),
        out_specs=[spec] * len(messages),
        out_shape=[pltpu.HBM(m.shape, m.dtype) for m in messages],
        input_output_aliases={i: i for i in range(len(messages))},
        compiler_params=pltpu.CompilerParams(vmem_limit_bytes=VMEM_BYTES),
    )(*map(kept, messages), *map(kept, after))


def per_device(voltages, coeffs):
    freq_count = lax.axis_size("freq")
    parts = lax.axis_size("inp") * freq_count
    inputs, frames, _ = voltages.shape
    width = CH // parts
    fits = (
        inputs == BLK
        and frames == 2 * TBLK
        and TBLK % TAPS == 0
        and parts & (parts - 1) == 0
        and parts >= 16
        and width % 16 == 0
        and parts * BLK == INPUTS * freq_count
        and freq_count * frames * 2 == LANES
    )
    if not fits:
        return any_sizes(voltages, coeffs)
    axes = ("inp", "freq")
    me = lax.axis_index("inp") * freq_count + lax.axis_index("freq")
    me = me.astype(jnp.int32).reshape(1)
    half = width // 2
    tables = parity_tables(parts, width)
    sizes = [width * 7 // 16, width * 9 // 16]
    starts = [0, sizes[0]]

    far, near = list(range(parts // 2, parts)), list(range(1, parts // 2))
    far = [s for pair in zip(far[: parts // 4], far[parts // 4 :]) for s in pair]
    near = near[parts // 4 - 1 :] + near[: parts // 4 - 1]
    log, passed = [], []

    def send(chunk, s, after=()):
        waits = list(after) + (log[-FLIGHT:][:1] if len(log) >= FLIGHT else [])
        message = messages[chunk][s]
        if waits:
            (message,) = gated(f"gate_{chunk}_{s}", [message], waits + passed)
            passed[:] = [message]
        arrived[chunk][s] = lax.ppermute(message, axes, [(i, i ^ s) for i in range(parts)])
        log.append(arrived[chunk][s])

    made = front(
        1,
        parts,
        me,
        voltages,
        coeffs,
        tables,
        [(width * 2 * TBLK, BLK)] * parts,
        lambda s, parity, channel: (s, parity * half + channel),
    )
    messages, arrived = [made[:parts]], [{0: made[0]}]
    history, earlier = made[parts], made[parts + 1]
    history = passed_along(history, "freq", 1)
    log.append(history)
    for s in far[: FLIGHT - 1]:
        send(0, s)

    def where(s, parity, channel):
        place = parity * half + channel
        chunk = max(i for i in range(len(starts)) if starts[i] <= place)
        return chunk * parts + s, place - starts[chunk]

    shapes = [(size * 2 * TBLK + (TBLK if i == 0 else 0), BLK) for i, size in enumerate(sizes)]
    made = front(
        0,
        parts,
        me,
        voltages,
        coeffs,
        tables,
        [shape for shape in shapes for _ in range(parts)],
        where,
        history,
        earlier,
    )
    for i in range(len(sizes)):
        messages.append(made[i * parts : (i + 1) * parts])
        arrived.append({0: made[i * parts]})
    done = [made[-1]]

    far_left = [(0, s) for s in far[FLIGHT - 1 :]] + [(1, s) for s in far]
    near_left = [(0, s) for s in near] + [(1, s) for s in near]
    lead = len(near_left) - len(far_left)
    while far_left or near_left:
        take = [near_left.pop(0)] if near_left else []
        if lead > 0 and near_left and len(far_left) % 4 == 0:
            take.append(near_left.pop(0))
            lead -= 1
        if far_left:
            take.append(far_left.pop(0))
        for chunk, s in take:
            send(chunk, s, done)

    def every(chunk):
        return [arrived[chunk][s] for s in range(parts)]

    out, token = None, done[0]
    for chunk in range(1, len(sizes) + 1):
        size, start = sizes[chunk - 1], starts[chunk - 1]
        if chunk == len(sizes):
            pieces = [size]
        else:
            pieces = [size - size // 2, size // 2]
            far_left, near_left = list(far), near[parts // 4 :] + near[: parts // 4]
            for s in far_left[: FLIGHT - 1]:
                send(chunk + 1, s, [token])
            far_left = far_left[FLIGHT - 1 :]
        after = []
        for index, count in enumerate(pieces):
            first = sum(pieces[:index])
            out, token = correlated(
                f"correlate_{chunk}_{index}",
                me,
                every(0),
                every(chunk),
                every(1),
                (start + first, first),
                count,
                width,
                out,
                after,
            )
            if chunk == len(sizes):
                break
            final = index == len(pieces) - 1
            first_near = near_left[0]
            for turn in range(len(near_left) if final else 3):
                if near_left:
                    send(chunk + 1, near_left.pop(0), [token])
                if far_left and turn < (len(near) if final else 2):
                    send(chunk + 1, far_left.pop(0), [token])
            after = [arrived[chunk + 1][first_near]]
    return out


def solution(mesh):
    in_specs = (P(("grp", "inp"), "freq", None), P())
    out_specs = P(("grp", "inp", "freq"), None, None, None, None)
    return jax.shard_map(
        per_device, mesh=mesh, in_specs=in_specs, out_specs=out_specs, check_vma=False
    )
```

```python
import math

import jax
import jax.numpy as jnp
import ml_dtypes
import numpy as np
from jax import lax
from jax.experimental import pallas as pl
from jax.experimental.pallas import tpu as pltpu
from jax.sharding import PartitionSpec as P

SPF = 2048
TAPS = 8
CH = 512
CH0 = 256
INPUTS = 1024
BLK = 128
LANES = 128
UBLK = 16
TBLK = 16
VMEM_BYTES = 64 * 2**20 - 2**16
FLIGHT = 5
PITCH = TBLK + 1


def passed_along(x, axis, by):
    length = lax.axis_size(axis)
    pairs = [(i, i + by) for i in range(length) if 0 <= i + by < length]
    return lax.ppermute(x, axis, pairs)


def make_table():
    sample = jnp.arange(SPF, dtype=jnp.int32)[:, None]
    channel = jnp.arange(CH, dtype=jnp.int32)[None, :] + CH0
    phase = sample * channel % SPF
    angle = phase.astype(jnp.float32) * (2.0 * math.pi / SPF)
    return jnp.concatenate([jnp.cos(angle), -jnp.sin(angle)], axis=1).astype(jnp.bfloat16)


def any_sizes(voltages, coeffs):
    inputs_here = voltages.shape[0]
    frames_here = voltages.shape[1]
    inp_count = lax.axis_size("inp")
    freq_count = lax.axis_size("freq")
    frames_all = frames_here * freq_count
    history = voltages[:, frames_here - (TAPS - 1) :, :].astype(jnp.bfloat16)
    earlier = passed_along(history, "freq", 1)
    extended = jnp.concatenate([earlier.astype(jnp.float32), voltages.astype(jnp.float32)], axis=1)
    weights = coeffs.astype(jnp.float32)
    summed = jnp.zeros((inputs_here, frames_here, SPF), jnp.float32)
    for tap_index in range(TAPS):
        begin = TAPS - 1 - tap_index
        summed = summed + weights[tap_index] * extended[:, begin : begin + frames_here, :]
    filtered = summed.astype(jnp.bfloat16).reshape(inputs_here * frames_here, SPF)
    spectrum_t = jnp.einsum("nj,rn->jr", make_table(), filtered, preferred_element_type=jnp.float32)
    spectrum_t = spectrum_t.reshape(2 * CH, inputs_here, frames_here)
    squares = jnp.sum(spectrum_t * spectrum_t, axis=(0, 2))
    power = lax.psum(squares, "freq") / (frames_all * CH)
    gains = 1.0 / jnp.sqrt(power + 1e-06)
    scaled = (spectrum_t * gains[None, :, None]).astype(jnp.bfloat16)
    scaled = scaled.reshape(2, CH, inputs_here * frames_here)
    arrived = lax.all_to_all(scaled[None], ("inp", "freq"), split_axis=2, concat_axis=0, tiled=True)
    width_here = arrived.shape[-2]
    arranged = arrived.reshape(inp_count, freq_count, 2, width_here, inputs_here, frames_here)
    arranged = jnp.transpose(arranged, (3, 0, 4, 2, 1, 5))
    stacked = arranged.reshape(width_here, INPUTS, 2 * frames_all)
    other = jnp.concatenate([-stacked[:, :, frames_all:], stacked[:, :, :frames_all]], axis=2)
    block_count = INPUTS // BLK
    scale = 1.0 / frames_all
    pieces = []
    for row_index in range(block_count):
        row_panel = stacked[:, row_index * BLK : (row_index + 1) * BLK]
        real_part = jnp.einsum(
            "cut,cmt->cum",
            row_panel,
            stacked[:, row_index * BLK :],
            preferred_element_type=jnp.float32,
        )
        imag_part = jnp.einsum(
            "cut,cmt->cum",
            row_panel,
            other[:, row_index * BLK :],
            preferred_element_type=jnp.float32,
        )
        band = jnp.stack([real_part, imag_part], axis=1) * scale
        for col_index in range(row_index, block_count):
            begin = (col_index - row_index) * BLK
            pieces.append(band[:, :, :, begin : begin + BLK])
    return jnp.stack(pieces, axis=2).astype(jnp.bfloat16)


def turned_over(rows):
    rows = list(rows)
    place = lax.broadcasted_iota(jnp.int32, (8, LANES), 0)
    for shift in (4, 2, 1):
        low = jnp.bitwise_and(place, shift) == 0
        for i in range(8):
            if i & shift == 0:
                near, far = rows[i], rows[i + shift]
                rows[i] = jnp.where(low, near, pltpu.roll(far, shift, 0))
                rows[i + shift] = jnp.where(low, pltpu.roll(near, 8 - shift, 0), far)
    return rows


def frames_of(v_ref, cols):
    groups = []
    for group in range(UBLK // 8):
        groups.append(turned_over([v_ref[group * 8 + i, :, cols] for i in range(8)]))
    return [[group[t].astype(jnp.float32) for group in groups] for t in range(8)]


def kept(array):
    return pltpu.with_memory_space_constraint(array, pltpu.HBM)


def parity_tables(parts, width):
    tables = []
    for parity in range(2):
        within = np.arange(parity, width, 2)
        channel = (np.arange(parts)[:, None] * width + within[None, :]).reshape(-1) + CH0
        phase = channel[:, None].astype(np.int64) * np.arange(SPF // 2)[None, :] % SPF
        angle = phase.astype(np.float32) * np.float32(2.0 * math.pi / SPF)
        wide = angle.astype(np.float64)
        both = np.stack([np.cos(wide), -np.sin(wide)], axis=1)
        both = both.reshape(-1, SPF // 2).astype(np.float32)
        tables.append(jnp.asarray(both.astype(ml_dtypes.bfloat16)))
    return tables


def filter_step(block, sources, c_ref, even, odd, last_ref):
    half = SPF // 2
    groups = UBLK // 8
    here = pl.ds(pl.multiple_of(pl.program_id(0) * UBLK, UBLK), UBLK)

    def column(step, carry):
        sides = []
        before = []
        for side in range(2):
            cols = pl.ds(pl.multiple_of(step * LANES + side * half, LANES), LANES)
            weights = c_ref[:, cols].astype(jnp.float32)
            taps = [jnp.broadcast_to(weights[k : k + 1], (8, LANES)) for k in range(TAPS)]
            sides.append((cols, taps))
            if block == 0:
                wide = [sources[0][t, :, cols].astype(jnp.float32) for t in range(TAPS)]
                before.append([[w[g * 8 : (g + 1) * 8] for g in range(groups)] for w in wide])
            else:
                before.append(frames_of(sources[0], cols))
        out = pl.ds(pl.multiple_of(step * LANES, LANES), LANES)
        for part in range(TBLK // TAPS):
            made = []
            for side, (cols, taps) in enumerate(sides):
                now = frames_of(sources[1 + part], cols)
                window = before[side] + now
                before[side] = now
                totals = []
                for t in range(TAPS):
                    frame = []
                    for g in range(groups):
                        total = taps[0] * window[TAPS + t][g]
                        for k in range(1, TAPS):
                            total = total + taps[k] * window[TAPS + t - k][g]
                        frame.append(total)
                    totals.append(jnp.concatenate(frame, axis=0))
                made.append(totals)
                if last_ref is not None and part == TBLK // TAPS - 1:
                    for t in range(TAPS):
                        frame = jnp.concatenate(now[t], axis=0)
                        last_ref[t, :, cols] = frame.astype(jnp.bfloat16)
            for t in range(TAPS):
                at = part * TAPS + t
                even[at, here, out] = (made[0][t] + made[1][t]).astype(jnp.bfloat16)
                odd[at, here, out] = (made[0][t] - made[1][t]).astype(jnp.bfloat16)
        return carry

    lax.fori_loop(0, half // LANES, column, 0)


def front_kernel(block, parts, where, me_ref, *refs):
    count = 1 + TBLK // TAPS
    sources, c_ref, tables = refs[:count], refs[count], refs[count + 1 : count + 3]
    earlier_ref = refs[count + 3] if block == 0 else None
    outs = refs[count + (4 if block == 0 else 3) : -4]
    last_ref = None if block == 0 else outs[-1]
    power_ref, even, odd, turned = refs[-4:]
    filter_step(block, sources, c_ref, even, odd, last_ref)

    @pl.when(pl.program_id(0) == pl.num_programs(0) - 1)
    def _():
        me = me_ref[0]
        square = jnp.zeros((8, BLK), jnp.float32)
        for parity, filtered in enumerate((even, odd)):
            rows = tables[parity].shape[0]
            own = rows // parts
            spectrum = lax.dot_general(
                tables[parity][...],
                filtered[...].reshape(-1, SPF // 2),
                (((1,), (1,)), ((), ())),
                preferred_element_type=jnp.float32,
            )
            for t in range(TBLK):
                frame = spectrum[:, t * BLK : (t + 1) * BLK]
                turned[pl.ds(t, rows, stride=PITCH), :] = frame
                square = square + jnp.sum((frame * frame).reshape(rows // 8, 8, BLK), axis=0)
            for s in range(parts):
                begin = jnp.bitwise_xor(me, s) * (own * PITCH)
                for channel in range(own // 2):
                    index, place = where(s, parity, channel)
                    for half in range(2):
                        row = channel * 2 + half
                        value = turned[pl.ds(begin + row * PITCH, TBLK), :].astype(jnp.bfloat16)
                        to = (place * 2 + half) * TBLK
                        outs[index][to : to + TBLK, :] = value
        if block == 0:
            square = square + earlier_ref[...]
            rest = jnp.sum(square, axis=0, keepdims=True)
            terms = []
            for _ in range(3):
                term = rest.astype(jnp.bfloat16).astype(jnp.float32)
                terms.append(term)
                rest = rest - term
            terms.append(jnp.zeros((TBLK - 3, BLK), jnp.float32))
            tail = jnp.concatenate(terms, axis=0).astype(jnp.bfloat16)
            for s in range(parts):
                size = outs[s].shape[0]
                outs[s][size - TBLK :, :] = tail
        power_ref[...] = square


def front(block, parts, me, voltages, coeffs, tables, shapes, where, history=None, earlier=None):
    inputs, frames, _ = voltages.shape
    half = SPF // 2
    first = block * (TBLK // TAPS)
    in_specs, operands = [], []
    for place in range(first - 1, first + TBLK // TAPS):
        if place < 0:
            in_specs.append(pl.BlockSpec((TAPS, UBLK, SPF), lambda i, me: (0, i, 0)))
            operands.append(kept(history))
        else:
            in_specs.append(
                pl.BlockSpec((UBLK, TAPS, SPF), lambda i, me, place=place: (i, place, 0))
            )
            operands.append(voltages)
    operands += [coeffs, *tables]
    if block == 0:
        operands.append(earlier)
    for array in operands[len(in_specs) :]:
        in_specs.append(pl.BlockSpec(array.shape, lambda i, me: (0, 0)))
    out_shapes = [pltpu.HBM(shape, jnp.bfloat16) for shape in shapes]
    out_specs = [pl.BlockSpec(shape, lambda i, me: (0, 0)) for shape in shapes]
    if block == 1:
        out_shapes.append(pltpu.HBM((TAPS, inputs, SPF), jnp.bfloat16))
        out_specs.append(pl.BlockSpec((TAPS, UBLK, SPF), lambda i, me: (0, i, 0)))
    out_shapes.append(jax.ShapeDtypeStruct((8, BLK), jnp.float32))
    out_specs.append(pl.BlockSpec((8, BLK), lambda i, me: (0, 0)))

    def kernel(me_ref, *refs):
        front_kernel(block, parts, where, me_ref, *refs)

    return pl.pallas_call(
        kernel,
        name=f"front_{block}",
        grid_spec=pltpu.PrefetchScalarGridSpec(
            num_scalar_prefetch=1,
            grid=(inputs // UBLK,),
            in_specs=in_specs,
            out_specs=out_specs,
            scratch_shapes=[
                pltpu.VMEM((TBLK, inputs, half), jnp.bfloat16),
                pltpu.VMEM((TBLK, inputs, half), jnp.bfloat16),
                pltpu.VMEM((tables[0].shape[0] * PITCH + 8, BLK), jnp.float32),
            ],
        ),
        out_shape=out_shapes,
        compiler_params=pltpu.CompilerParams(vmem_limit_bytes=VMEM_BYTES),
    )(me, *operands)


def correlate_kernel(parts, first, count, me_ref, *refs):
    late, early, powers = refs[:parts], refs[parts : 2 * parts], refs[2 * parts : 3 * parts]
    out_ref, token_ref, plain, other, columns, lines, shares, ready, sems = refs[-9:]
    blocks = INPUTS // BLK
    freq = parts // blocks
    me = me_ref[0]

    step = pl.program_id(0)
    slot = lax.rem(step, 2)
    depth = out_ref.shape[0]

    def writes(step, slot):
        channel = 2 * lax.rem(first + step, depth // 2) + lax.div(first + step, depth // 2)
        return [
            pltpu.make_async_copy(
                ready.at[slot, part], out_ref.at[channel, part], sems.at[slot, part]
            )
            for part in range(2)
        ]

    @pl.when(step >= 2)
    def _():
        for write in writes(step - 2, slot):
            write.wait()

    @pl.when(step == 0)
    def _():
        token_ref[...] = jnp.zeros_like(token_ref)
        for s in range(parts):
            terms = powers[s][...].astype(jnp.float32)
            power = terms[0:1] + terms[1:2] + terms[2:3]
            shares[jnp.bitwise_xor(me, s)] = jnp.broadcast_to(power, (8, BLK))
        for r in range(blocks):
            power = shares[r * freq]
            for f in range(1, freq):
                power = power + shares[r * freq + f]
            gain = 1.0 / jnp.sqrt(power / (freq * 2 * TBLK * CH) + 1e-06)
            lines[r] = gain
            columns[r * BLK : (r + 1) * BLK, :] = jnp.broadcast_to(gain[0:1], (BLK, BLK)).T

    for s in range(parts):
        source = jnp.bitwise_xor(me, s)
        block, place = source // freq, source % freq
        for half, ref in enumerate((late[s], early[s])):
            begin = pl.multiple_of((place * 2 + half) * 2 * TBLK, 2 * TBLK)
            real = ref[:TBLK, :]
            imag = ref[TBLK:, :]
            plain[block, pl.ds(begin, TBLK), :] = real
            plain[block, pl.ds(begin + TBLK, TBLK), :] = imag
            other[block, pl.ds(begin, TBLK), :] = -imag
            other[block, pl.ds(begin + TBLK, TBLK), :] = real

    sides = [plain[r].T for r in range(blocks)]
    for c in range(blocks):
        weights = jnp.concatenate([plain[c], other[c]], axis=1)
        line = lines[c][0:1] * (1.0 / (freq * 2 * TBLK))
        for r in range(c + 1):
            both = jnp.dot(sides[r], weights, preferred_element_type=jnp.float32)
            pair = r * blocks - r * (r - 1) // 2 + (c - r)
            gain = columns[r * BLK : (r + 1) * BLK, :] * line
            for part in range(2):
                piece = both[:, part * BLK : (part + 1) * BLK]
                ready[slot, part, pair] = (piece * gain).astype(jnp.bfloat16)

    for write in writes(step, slot):
        write.start()

    @pl.when(step == count - 1)
    def _():
        if count > 1:
            for write in writes(step - 1, 1 - slot):
                write.wait()
        for write in writes(step, slot):
            write.wait()


def correlated(name, me, late, early, powers, spot, count, width, before, after=()):
    parts = len(late)
    blocks = INPUTS // BLK
    pairs = blocks * (blocks + 1) // 2
    span = parts // blocks * 4 * TBLK
    first, second = spot
    last = powers[0].shape[0] // TBLK - 1
    in_specs = (
        [pl.BlockSpec((2 * TBLK, BLK), lambda i, me: (first + i, 0))] * parts
        + [pl.BlockSpec((2 * TBLK, BLK), lambda i, me: (second + i, 0))] * parts
        + [pl.BlockSpec((TBLK, BLK), lambda i, me: (last, 0))] * parts
    )
    operands = [me, *map(kept, late), *map(kept, early), *map(kept, powers)]
    aliases = {}
    if before is not None:
        aliases[len(operands)] = 0
        operands.append(before)
    operands += map(kept, after)
    in_specs += [pl.BlockSpec(memory_space=pl.ANY)] * (len(operands) - 1 - len(in_specs))

    def kernel(me_ref, *refs):
        correlate_kernel(parts, first, count, me_ref, *refs)

    return pl.pallas_call(
        kernel,
        name=name,
        grid_spec=pltpu.PrefetchScalarGridSpec(
            num_scalar_prefetch=1,
            grid=(count,),
            in_specs=in_specs,
            out_specs=[
                pl.BlockSpec(memory_space=pl.ANY),
                pl.BlockSpec((8, BLK), lambda i, me: (0, 0)),
            ],
            scratch_shapes=[
                pltpu.VMEM((blocks, span, BLK), jnp.bfloat16),
                pltpu.VMEM((blocks, span, BLK), jnp.bfloat16),
                pltpu.VMEM((INPUTS, BLK), jnp.float32),
                pltpu.VMEM((blocks, 8, BLK), jnp.float32),
                pltpu.VMEM((parts, 8, BLK), jnp.float32),
                pltpu.VMEM((2, 2, pairs, BLK, BLK), jnp.bfloat16),
                pltpu.SemaphoreType.DMA((2, 2)),
            ],
        ),
        out_shape=[
            jax.ShapeDtypeStruct((width, 2, pairs, BLK, BLK), jnp.bfloat16),
            jax.ShapeDtypeStruct((8, BLK), jnp.float32),
        ],
        input_output_aliases=aliases,
        compiler_params=pltpu.CompilerParams(vmem_limit_bytes=VMEM_BYTES),
    )(*operands)


def nothing_kernel(*refs):
    del refs


def gated(name, messages, after):
    spec = pl.BlockSpec(memory_space=pl.ANY)
    return pl.pallas_call(
        nothing_kernel,
        name=name,
        in_specs=[spec] * (len(messages) + len(after)),
        out_specs=[spec] * len(messages),
        out_shape=[pltpu.HBM(m.shape, m.dtype) for m in messages],
        input_output_aliases={i: i for i in range(len(messages))},
        compiler_params=pltpu.CompilerParams(vmem_limit_bytes=VMEM_BYTES),
    )(*map(kept, messages), *map(kept, after))


def per_device(voltages, coeffs):
    freq_count = lax.axis_size("freq")
    parts = lax.axis_size("inp") * freq_count
    inputs, frames, _ = voltages.shape
    width = CH // parts
    fits = (
        inputs == BLK
        and frames == 2 * TBLK
        and TBLK % TAPS == 0
        and parts & (parts - 1) == 0
        and parts >= 16
        and width % 16 == 0
        and parts * BLK == INPUTS * freq_count
        and freq_count * frames * 2 == LANES
    )
    if not fits:
        return any_sizes(voltages, coeffs)
    axes = ("inp", "freq")
    me = lax.axis_index("inp") * freq_count + lax.axis_index("freq")
    me = me.astype(jnp.int32).reshape(1)
    half = width // 2
    tables = parity_tables(parts, width)
    sizes = [width * 7 // 16, width * 9 // 16]
    starts = [0, sizes[0]]

    far, near = list(range(parts // 2, parts)), list(range(1, parts // 2))
    far = [s for pair in zip(far[: parts // 4], far[parts // 4 :]) for s in pair]
    near = near[parts // 4 - 1 :] + near[: parts // 4 - 1]
    log, passed = [], []

    def send(chunk, s, after=()):
        waits = list(after) + (log[-FLIGHT:][:1] if len(log) >= FLIGHT else [])
        message = messages[chunk][s]
        if waits:
            (message,) = gated(f"gate_{chunk}_{s}", [message], waits + passed)
            passed[:] = [message]
        arrived[chunk][s] = lax.ppermute(message, axes, [(i, i ^ s) for i in range(parts)])
        log.append(arrived[chunk][s])

    made = front(
        1,
        parts,
        me,
        voltages,
        coeffs,
        tables,
        [(width * 2 * TBLK, BLK)] * parts,
        lambda s, parity, channel: (s, parity * half + channel),
    )
    messages, arrived = [made[:parts]], [{0: made[0]}]
    history, earlier = made[parts], made[parts + 1]
    history = passed_along(history, "freq", 1)
    log.append(history)
    for s in far[: FLIGHT - 1]:
        send(0, s)

    def where(s, parity, channel):
        place = parity * half + channel
        chunk = max(i for i in range(len(starts)) if starts[i] <= place)
        return chunk * parts + s, place - starts[chunk]

    shapes = [(size * 2 * TBLK + (TBLK if i == 0 else 0), BLK) for i, size in enumerate(sizes)]
    made = front(
        0,
        parts,
        me,
        voltages,
        coeffs,
        tables,
        [shape for shape in shapes for _ in range(parts)],
        where,
        history,
        earlier,
    )
    for i in range(len(sizes)):
        messages.append(made[i * parts : (i + 1) * parts])
        arrived.append({0: made[i * parts]})
    done = [made[-1]]

    far_left = [(0, s) for s in far[FLIGHT - 1 :]] + [(1, s) for s in far]
    near_left = [(0, s) for s in near] + [(1, s) for s in near]
    lead = len(near_left) - len(far_left)
    while far_left or near_left:
        take = [near_left.pop(0)] if near_left else []
        if lead > 0 and near_left and len(far_left) % 4 == 0:
            take.append(near_left.pop(0))
            lead -= 1
        if far_left:
            take.append(far_left.pop(0))
        for chunk, s in take:
            send(chunk, s, done)

    def every(chunk):
        return [arrived[chunk][s] for s in range(parts)]

    out, token = None, done[0]
    for chunk in range(1, len(sizes) + 1):
        size, start = sizes[chunk - 1], starts[chunk - 1]
        if chunk == len(sizes):
            pieces = [size]
        else:
            pieces = [size - size // 2, size // 2]
            far_left, near_left = list(far), near[parts // 4 :] + near[: parts // 4]
            for s in far_left[: FLIGHT - 1]:
                send(chunk + 1, s, [token])
            far_left = far_left[FLIGHT - 1 :]
        after = []
        for index, count in enumerate(pieces):
            first = sum(pieces[:index])
            out, token = correlated(
                f"correlate_{chunk}_{index}",
                me,
                every(0),
                every(chunk),
                every(1),
                (start + first, first),
                count,
                width,
                out,
                after,
            )
            if chunk == len(sizes):
                break
            if index == len(pieces) - 1:
                turns = [near_left.pop(0) for _ in range(len(near_left))]
                turns = far_left + turns
            else:
                near_now = [near_left.pop(0) for _ in range(parts // 4 - 1)]
                turns = []
                for near_one in near_now:
                    turns += [near_one, far_left.pop(0)]
                turns = turns[:-2] + [turns[-1], turns[-2]] + far_left
                far_left = []
            for s in turns:
                send(chunk + 1, s, [token])
            after = [arrived[chunk + 1][turns[1]], arrived[chunk + 1][turns[-2]]]
    return out


def solution(mesh):
    in_specs = (P(("grp", "inp"), "freq", None), P())
    out_specs = P(("grp", "inp", "freq"), None, None, None, None)
    return jax.shard_map(
        per_device, mesh=mesh, in_specs=in_specs, out_specs=out_specs, check_vma=False
    )
```

```python
import math

import jax
import jax.numpy as jnp
import ml_dtypes
import numpy as np
from jax import lax
from jax.experimental import pallas as pl
from jax.experimental.pallas import tpu as pltpu
from jax.sharding import PartitionSpec as P

SPF = 2048
TAPS = 8
CH = 512
CH0 = 256
INPUTS = 1024
BLK = 128
LANES = 128
UBLK = 16
TBLK = 16
VMEM_BYTES = 64 * 2**20 - 2**16
FLIGHT = 5
PITCH = TBLK + 1


def passed_along(x, axis, by):
    length = lax.axis_size(axis)
    pairs = [(i, i + by) for i in range(length) if 0 <= i + by < length]
    return lax.ppermute(x, axis, pairs)


def make_table():
    sample = jnp.arange(SPF, dtype=jnp.int32)[:, None]
    channel = jnp.arange(CH, dtype=jnp.int32)[None, :] + CH0
    phase = sample * channel % SPF
    angle = phase.astype(jnp.float32) * (2.0 * math.pi / SPF)
    return jnp.concatenate([jnp.cos(angle), -jnp.sin(angle)], axis=1).astype(jnp.bfloat16)


def any_sizes(voltages, coeffs):
    inputs_here = voltages.shape[0]
    frames_here = voltages.shape[1]
    inp_count = lax.axis_size("inp")
    freq_count = lax.axis_size("freq")
    frames_all = frames_here * freq_count
    history = voltages[:, frames_here - (TAPS - 1) :, :].astype(jnp.bfloat16)
    earlier = passed_along(history, "freq", 1)
    extended = jnp.concatenate([earlier.astype(jnp.float32), voltages.astype(jnp.float32)], axis=1)
    weights = coeffs.astype(jnp.float32)
    summed = jnp.zeros((inputs_here, frames_here, SPF), jnp.float32)
    for tap_index in range(TAPS):
        begin = TAPS - 1 - tap_index
        summed = summed + weights[tap_index] * extended[:, begin : begin + frames_here, :]
    filtered = summed.astype(jnp.bfloat16).reshape(inputs_here * frames_here, SPF)
    spectrum_t = jnp.einsum("nj,rn->jr", make_table(), filtered, preferred_element_type=jnp.float32)
    spectrum_t = spectrum_t.reshape(2 * CH, inputs_here, frames_here)
    squares = jnp.sum(spectrum_t * spectrum_t, axis=(0, 2))
    power = lax.psum(squares, "freq") / (frames_all * CH)
    gains = 1.0 / jnp.sqrt(power + 1e-06)
    scaled = (spectrum_t * gains[None, :, None]).astype(jnp.bfloat16)
    scaled = scaled.reshape(2, CH, inputs_here * frames_here)
    arrived = lax.all_to_all(scaled[None], ("inp", "freq"), split_axis=2, concat_axis=0, tiled=True)
    width_here = arrived.shape[-2]
    arranged = arrived.reshape(inp_count, freq_count, 2, width_here, inputs_here, frames_here)
    arranged = jnp.transpose(arranged, (3, 0, 4, 2, 1, 5))
    stacked = arranged.reshape(width_here, INPUTS, 2 * frames_all)
    other = jnp.concatenate([-stacked[:, :, frames_all:], stacked[:, :, :frames_all]], axis=2)
    block_count = INPUTS // BLK
    scale = 1.0 / frames_all
    pieces = []
    for row_index in range(block_count):
        row_panel = stacked[:, row_index * BLK : (row_index + 1) * BLK]
        real_part = jnp.einsum(
            "cut,cmt->cum",
            row_panel,
            stacked[:, row_index * BLK :],
            preferred_element_type=jnp.float32,
        )
        imag_part = jnp.einsum(
            "cut,cmt->cum",
            row_panel,
            other[:, row_index * BLK :],
            preferred_element_type=jnp.float32,
        )
        band = jnp.stack([real_part, imag_part], axis=1) * scale
        for col_index in range(row_index, block_count):
            begin = (col_index - row_index) * BLK
            pieces.append(band[:, :, :, begin : begin + BLK])
    return jnp.stack(pieces, axis=2).astype(jnp.bfloat16)


def turned_over(rows):
    rows = list(rows)
    place = lax.broadcasted_iota(jnp.int32, (8, LANES), 0)
    for shift in (4, 2, 1):
        low = jnp.bitwise_and(place, shift) == 0
        for i in range(8):
            if i & shift == 0:
                near, far = rows[i], rows[i + shift]
                rows[i] = jnp.where(low, near, pltpu.roll(far, shift, 0))
                rows[i + shift] = jnp.where(low, pltpu.roll(near, 8 - shift, 0), far)
    return rows


def frames_of(v_ref, cols):
    groups = []
    for group in range(UBLK // 8):
        groups.append(turned_over([v_ref[group * 8 + i, :, cols] for i in range(8)]))
    return [[group[t].astype(jnp.float32) for group in groups] for t in range(8)]


def kept(array):
    return pltpu.with_memory_space_constraint(array, pltpu.HBM)


def parity_tables(parts, width):
    tables = []
    for parity in range(2):
        within = np.arange(parity, width, 2)
        channel = (np.arange(parts)[:, None] * width + within[None, :]).reshape(-1) + CH0
        phase = channel[:, None].astype(np.int64) * np.arange(SPF // 2)[None, :] % SPF
        angle = phase.astype(np.float32) * np.float32(2.0 * math.pi / SPF)
        wide = angle.astype(np.float64)
        both = np.stack([np.cos(wide), -np.sin(wide)], axis=1)
        both = both.reshape(-1, SPF // 2).astype(np.float32)
        tables.append(jnp.asarray(both.astype(ml_dtypes.bfloat16)))
    return tables


def filter_step(block, sources, c_ref, even, odd, last_ref):
    half = SPF // 2
    groups = UBLK // 8
    here = pl.ds(pl.multiple_of(pl.program_id(0) * UBLK, UBLK), UBLK)

    def column(step, carry):
        sides = []
        before = []
        for side in range(2):
            cols = pl.ds(pl.multiple_of(step * LANES + side * half, LANES), LANES)
            weights = c_ref[:, cols].astype(jnp.float32)
            taps = [jnp.broadcast_to(weights[k : k + 1], (8, LANES)) for k in range(TAPS)]
            sides.append((cols, taps))
            if block == 0:
                wide = [sources[0][t, :, cols].astype(jnp.float32) for t in range(TAPS)]
                before.append([[w[g * 8 : (g + 1) * 8] for g in range(groups)] for w in wide])
            else:
                before.append(frames_of(sources[0], cols))
        out = pl.ds(pl.multiple_of(step * LANES, LANES), LANES)
        for part in range(TBLK // TAPS):
            made = []
            for side, (cols, taps) in enumerate(sides):
                now = frames_of(sources[1 + part], cols)
                window = before[side] + now
                before[side] = now
                totals = []
                for t in range(TAPS):
                    frame = []
                    for g in range(groups):
                        total = taps[0] * window[TAPS + t][g]
                        for k in range(1, TAPS):
                            total = total + taps[k] * window[TAPS + t - k][g]
                        frame.append(total)
                    totals.append(jnp.concatenate(frame, axis=0))
                made.append(totals)
                if last_ref is not None and part == TBLK // TAPS - 1:
                    for t in range(TAPS):
                        frame = jnp.concatenate(now[t], axis=0)
                        last_ref[t, :, cols] = frame.astype(jnp.bfloat16)
            for t in range(TAPS):
                at = part * TAPS + t
                even[at, here, out] = (made[0][t] + made[1][t]).astype(jnp.bfloat16)
                odd[at, here, out] = (made[0][t] - made[1][t]).astype(jnp.bfloat16)
        return carry

    lax.fori_loop(0, half // LANES, column, 0)


def front_kernel(block, parts, where, me_ref, *refs):
    count = 1 + TBLK // TAPS
    sources, c_ref, tables = refs[:count], refs[count], refs[count + 1 : count + 3]
    earlier_ref = refs[count + 3] if block == 0 else None
    outs = refs[count + (4 if block == 0 else 3) : -4]
    last_ref = None if block == 0 else outs[-1]
    power_ref, even, odd, turned = refs[-4:]
    filter_step(block, sources, c_ref, even, odd, last_ref)

    @pl.when(pl.program_id(0) == pl.num_programs(0) - 1)
    def _():
        me = me_ref[0]
        square = jnp.zeros((8, BLK), jnp.float32)
        for parity, filtered in enumerate((even, odd)):
            rows = tables[parity].shape[0]
            own = rows // parts
            spectrum = lax.dot_general(
                tables[parity][...],
                filtered[...].reshape(-1, SPF // 2),
                (((1,), (1,)), ((), ())),
                preferred_element_type=jnp.float32,
            )
            for t in range(TBLK):
                frame = spectrum[:, t * BLK : (t + 1) * BLK]
                turned[pl.ds(t, rows, stride=PITCH), :] = frame
                square = square + jnp.sum((frame * frame).reshape(rows // 8, 8, BLK), axis=0)
            for s in range(parts):
                begin = jnp.bitwise_xor(me, s) * (own * PITCH)
                for channel in range(own // 2):
                    index, place = where(s, parity, channel)
                    for half in range(2):
                        row = channel * 2 + half
                        value = turned[pl.ds(begin + row * PITCH, TBLK), :].astype(jnp.bfloat16)
                        to = (place * 2 + half) * TBLK
                        outs[index][to : to + TBLK, :] = value
        if block == 0:
            square = square + earlier_ref[...]
            rest = jnp.sum(square, axis=0, keepdims=True)
            terms = []
            for _ in range(3):
                term = rest.astype(jnp.bfloat16).astype(jnp.float32)
                terms.append(term)
                rest = rest - term
            terms.append(jnp.zeros((TBLK - 3, BLK), jnp.float32))
            tail = jnp.concatenate(terms, axis=0).astype(jnp.bfloat16)
            for s in range(parts):
                size = outs[s].shape[0]
                outs[s][size - TBLK :, :] = tail
        power_ref[...] = square


def front(block, parts, me, voltages, coeffs, tables, shapes, where, history=None, earlier=None):
    inputs, frames, _ = voltages.shape
    half = SPF // 2
    first = block * (TBLK // TAPS)
    in_specs, operands = [], []
    for place in range(first - 1, first + TBLK // TAPS):
        if place < 0:
            in_specs.append(pl.BlockSpec((TAPS, UBLK, SPF), lambda i, me: (0, i, 0)))
            operands.append(kept(history))
        else:
            in_specs.append(
                pl.BlockSpec((UBLK, TAPS, SPF), lambda i, me, place=place: (i, place, 0))
            )
            operands.append(voltages)
    operands += [coeffs, *tables]
    if block == 0:
        operands.append(earlier)
    for array in operands[len(in_specs) :]:
        in_specs.append(pl.BlockSpec(array.shape, lambda i, me: (0, 0)))
    out_shapes = [pltpu.HBM(shape, jnp.bfloat16) for shape in shapes]
    out_specs = [pl.BlockSpec(shape, lambda i, me: (0, 0)) for shape in shapes]
    if block == 1:
        out_shapes.append(pltpu.HBM((TAPS, inputs, SPF), jnp.bfloat16))
        out_specs.append(pl.BlockSpec((TAPS, UBLK, SPF), lambda i, me: (0, i, 0)))
    out_shapes.append(jax.ShapeDtypeStruct((8, BLK), jnp.float32))
    out_specs.append(pl.BlockSpec((8, BLK), lambda i, me: (0, 0)))

    def kernel(me_ref, *refs):
        front_kernel(block, parts, where, me_ref, *refs)

    return pl.pallas_call(
        kernel,
        name=f"front_{block}",
        grid_spec=pltpu.PrefetchScalarGridSpec(
            num_scalar_prefetch=1,
            grid=(inputs // UBLK,),
            in_specs=in_specs,
            out_specs=out_specs,
            scratch_shapes=[
                pltpu.VMEM((TBLK, inputs, half), jnp.bfloat16),
                pltpu.VMEM((TBLK, inputs, half), jnp.bfloat16),
                pltpu.VMEM((tables[0].shape[0] * PITCH + 8, BLK), jnp.float32),
            ],
        ),
        out_shape=out_shapes,
        compiler_params=pltpu.CompilerParams(vmem_limit_bytes=VMEM_BYTES),
    )(me, *operands)


def correlate_kernel(parts, first, count, me_ref, *refs):
    late, early, powers = refs[:parts], refs[parts : 2 * parts], refs[2 * parts : 3 * parts]
    out_ref, token_ref, plain, other, columns, lines, shares, ready, sems = refs[-9:]
    blocks = INPUTS // BLK
    freq = parts // blocks
    me = me_ref[0]

    step = pl.program_id(0)
    slot = lax.rem(step, 2)
    depth = out_ref.shape[0]

    def writes(step, slot):
        channel = 2 * lax.rem(first + step, depth // 2) + lax.div(first + step, depth // 2)
        return [
            pltpu.make_async_copy(
                ready.at[slot, part], out_ref.at[channel, part], sems.at[slot, part]
            )
            for part in range(2)
        ]

    @pl.when(step >= 2)
    def _():
        for write in writes(step - 2, slot):
            write.wait()

    @pl.when(step == 0)
    def _():
        token_ref[...] = jnp.zeros_like(token_ref)
        for s in range(parts):
            terms = powers[s][...].astype(jnp.float32)
            power = terms[0:1] + terms[1:2] + terms[2:3]
            shares[jnp.bitwise_xor(me, s)] = jnp.broadcast_to(power, (8, BLK))
        for r in range(blocks):
            power = shares[r * freq]
            for f in range(1, freq):
                power = power + shares[r * freq + f]
            gain = 1.0 / jnp.sqrt(power / (freq * 2 * TBLK * CH) + 1e-06)
            lines[r] = gain
            columns[r * BLK : (r + 1) * BLK, :] = jnp.broadcast_to(gain[0:1], (BLK, BLK)).T

    for s in range(parts):
        source = jnp.bitwise_xor(me, s)
        block, place = source // freq, source % freq
        for half, ref in enumerate((late[s], early[s])):
            begin = pl.multiple_of((place * 2 + half) * 2 * TBLK, 2 * TBLK)
            real = ref[:TBLK, :]
            imag = ref[TBLK:, :]
            plain[block, pl.ds(begin, TBLK), :] = real
            plain[block, pl.ds(begin + TBLK, TBLK), :] = imag
            other[block, pl.ds(begin, TBLK), :] = -imag
            other[block, pl.ds(begin + TBLK, TBLK), :] = real

    sides = [plain[r].T for r in range(blocks)]
    for c in range(blocks):
        weights = jnp.concatenate([plain[c], other[c]], axis=1)
        line = lines[c][0:1] * (1.0 / (freq * 2 * TBLK))
        for r in range(c + 1):
            both = jnp.dot(sides[r], weights, preferred_element_type=jnp.float32)
            pair = r * blocks - r * (r - 1) // 2 + (c - r)
            gain = columns[r * BLK : (r + 1) * BLK, :] * line
            for part in range(2):
                piece = both[:, part * BLK : (part + 1) * BLK]
                ready[slot, part, pair] = (piece * gain).astype(jnp.bfloat16)

    for write in writes(step, slot):
        write.start()

    @pl.when(step == count - 1)
    def _():
        if count > 1:
            for write in writes(step - 1, 1 - slot):
                write.wait()
        for write in writes(step, slot):
            write.wait()


def correlated(name, me, late, early, powers, spot, count, width, before, after=()):
    parts = len(late)
    blocks = INPUTS // BLK
    pairs = blocks * (blocks + 1) // 2
    span = parts // blocks * 4 * TBLK
    first, second = spot
    last = powers[0].shape[0] // TBLK - 1
    in_specs = (
        [pl.BlockSpec((2 * TBLK, BLK), lambda i, me: (first + i, 0))] * parts
        + [pl.BlockSpec((2 * TBLK, BLK), lambda i, me: (second + i, 0))] * parts
        + [pl.BlockSpec((TBLK, BLK), lambda i, me: (last, 0))] * parts
    )
    operands = [me, *map(kept, late), *map(kept, early), *map(kept, powers)]
    aliases = {}
    if before is not None:
        aliases[len(operands)] = 0
        operands.append(before)
    operands += map(kept, after)
    in_specs += [pl.BlockSpec(memory_space=pl.ANY)] * (len(operands) - 1 - len(in_specs))

    def kernel(me_ref, *refs):
        correlate_kernel(parts, first, count, me_ref, *refs)

    return pl.pallas_call(
        kernel,
        name=name,
        grid_spec=pltpu.PrefetchScalarGridSpec(
            num_scalar_prefetch=1,
            grid=(count,),
            in_specs=in_specs,
            out_specs=[
                pl.BlockSpec(memory_space=pl.ANY),
                pl.BlockSpec((8, BLK), lambda i, me: (0, 0)),
            ],
            scratch_shapes=[
                pltpu.VMEM((blocks, span, BLK), jnp.bfloat16),
                pltpu.VMEM((blocks, span, BLK), jnp.bfloat16),
                pltpu.VMEM((INPUTS, BLK), jnp.float32),
                pltpu.VMEM((blocks, 8, BLK), jnp.float32),
                pltpu.VMEM((parts, 8, BLK), jnp.float32),
                pltpu.VMEM((2, 2, pairs, BLK, BLK), jnp.bfloat16),
                pltpu.SemaphoreType.DMA((2, 2)),
            ],
        ),
        out_shape=[
            jax.ShapeDtypeStruct((width, 2, pairs, BLK, BLK), jnp.bfloat16),
            jax.ShapeDtypeStruct((8, BLK), jnp.float32),
        ],
        input_output_aliases=aliases,
        compiler_params=pltpu.CompilerParams(vmem_limit_bytes=VMEM_BYTES),
    )(*operands)


def nothing_kernel(*refs):
    del refs


def gated(name, messages, after):
    spec = pl.BlockSpec(memory_space=pl.ANY)
    return pl.pallas_call(
        nothing_kernel,
        name=name,
        in_specs=[spec] * (len(messages) + len(after)),
        out_specs=[spec] * len(messages),
        out_shape=[pltpu.HBM(m.shape, m.dtype) for m in messages],
        input_output_aliases={i: i for i in range(len(messages))},
        compiler_params=pltpu.CompilerParams(vmem_limit_bytes=VMEM_BYTES),
    )(*map(kept, messages), *map(kept, after))


def per_device(voltages, coeffs):
    freq_count = lax.axis_size("freq")
    parts = lax.axis_size("inp") * freq_count
    inputs, frames, _ = voltages.shape
    width = CH // parts
    fits = (
        inputs == BLK
        and frames == 2 * TBLK
        and TBLK % TAPS == 0
        and parts & (parts - 1) == 0
        and parts >= 16
        and width % 16 == 0
        and parts * BLK == INPUTS * freq_count
        and freq_count * frames * 2 == LANES
    )
    if not fits:
        return any_sizes(voltages, coeffs)
    axes = ("inp", "freq")
    me = lax.axis_index("inp") * freq_count + lax.axis_index("freq")
    me = me.astype(jnp.int32).reshape(1)
    half = width // 2
    tables = parity_tables(parts, width)
    sizes = [width * 7 // 16, width * 9 // 16]
    starts = [0, sizes[0]]

    far, near = list(range(parts // 2, parts)), list(range(1, parts // 2))
    far = [s for pair in zip(far[: parts // 4], far[parts // 4 :]) for s in pair]
    near = near[parts // 4 - 1 :] + near[: parts // 4 - 1]
    log, passed = [], []

    def send(chunk, s, after=()):
        waits = list(after) + (log[-FLIGHT:][:1] if len(log) >= FLIGHT else [])
        message = messages[chunk][s]
        if waits:
            (message,) = gated(f"gate_{chunk}_{s}", [message], waits + passed)
            passed[:] = [message]
        arrived[chunk][s] = lax.ppermute(message, axes, [(i, i ^ s) for i in range(parts)])
        log.append(arrived[chunk][s])

    made = front(
        1,
        parts,
        me,
        voltages,
        coeffs,
        tables,
        [(width * 2 * TBLK, BLK)] * parts,
        lambda s, parity, channel: (s, parity * half + channel),
    )
    messages, arrived = [made[:parts]], [{0: made[0]}]
    history, earlier = made[parts], made[parts + 1]
    history = passed_along(history, "freq", 1)
    log.append(history)
    for s in far[: FLIGHT - 1]:
        send(0, s)

    def where(s, parity, channel):
        place = parity * half + channel
        chunk = max(i for i in range(len(starts)) if starts[i] <= place)
        return chunk * parts + s, place - starts[chunk]

    shapes = [(size * 2 * TBLK + (TBLK if i == 0 else 0), BLK) for i, size in enumerate(sizes)]
    made = front(
        0,
        parts,
        me,
        voltages,
        coeffs,
        tables,
        [shape for shape in shapes for _ in range(parts)],
        where,
        history,
        earlier,
    )
    for i in range(len(sizes)):
        messages.append(made[i * parts : (i + 1) * parts])
        arrived.append({0: made[i * parts]})
    done = [made[-1]]

    far_left = [(0, s) for s in far[FLIGHT - 1 :]] + [(1, s) for s in far]
    near_left = [(0, s) for s in near] + [(1, s) for s in near]
    lead = len(near_left) - len(far_left)
    while far_left or near_left:
        take = [near_left.pop(0)] if near_left else []
        if lead > 0 and near_left and len(far_left) % 4 == 0:
            take.append(near_left.pop(0))
            lead -= 1
        if far_left:
            take.append(far_left.pop(0))
        for chunk, s in take:
            send(chunk, s, done)

    def every(chunk):
        return [arrived[chunk][s] for s in range(parts)]

    out, token = None, done[0]
    for chunk in range(1, len(sizes) + 1):
        size, start = sizes[chunk - 1], starts[chunk - 1]
        if chunk == len(sizes):
            pieces = [size]
        else:
            pieces = [size]
            far_left, near_left = list(far), near[parts // 4 :] + near[: parts // 4]
            for s in far_left[: FLIGHT - 1]:
                send(chunk + 1, s, [token])
            far_left = far_left[FLIGHT - 1 :]
        after = []
        for index, count in enumerate(pieces):
            first = sum(pieces[:index])
            out, token = correlated(
                f"correlate_{chunk}_{index}",
                me,
                every(0),
                every(chunk),
                every(1),
                (start + first, first),
                count,
                width,
                out,
                after,
            )
            if chunk == len(sizes):
                break
            final = index == len(pieces) - 1
            first_near = near_left[0]
            for turn in range(len(near_left) if final else 3):
                if near_left:
                    send(chunk + 1, near_left.pop(0), [token])
                if far_left and turn < (len(near) if final else 2):
                    send(chunk + 1, far_left.pop(0), [token])
            after = [arrived[chunk + 1][first_near]]
    return out


def solution(mesh):
    in_specs = (P(("grp", "inp"), "freq", None), P())
    out_specs = P(("grp", "inp", "freq"), None, None, None, None)
    return jax.shard_map(
        per_device, mesh=mesh, in_specs=in_specs, out_specs=out_specs, check_vma=False
    )
```
